512 devices in a mesh: tm: 64 (over x, z, core), rows: 8 (over y).
Axes of the slice: x: 4, y: 8, z: 8, core: 2. Of those that a mesh axis runs over, the one named last changes fastest.
Arguments:
- returns: float32 [4096, 16384], P('tm', 'rows'), may hold values from -6 to 6
- variances: float32 [4096, 16384], P('tm', 'rows'), may hold values from 0.3 to 6
- loadings: float32 [16384], P('rows'), may hold values from -4 to 4
- sector: int32 [16384], P('rows'), may hold values from 0 to 511
- persistence: float32 [512], replicated, may hold values from 0.9 to 1, as said below
- factor_noise: float32 [4096, 512], P('tm'), may hold values from 0 to 200, as said below
Outputs:
- smoothed_mean: float32 [4096, 512], P('tm', 'rows')
- log_variance: float32 [4096, 512], P('tm', 'rows')
The draws below stay inside these ranges and needn't reach their ends.
Inputs may be any that keep to these rules, and one draw needn't show every extreme that they name: `persistence`: each coefficient lies strictly between 0 and 1. `factor_noise`: every entry is positive.
All inputs are finite; a program needn't handle non-finite values.
Results may differ from the reference program's by a relative error of at most 0.00065.
Values sent between devices are 32-bit elements; how exact they have to be, the bound alone decides.
No kernel may reach another device: no remote copies, remote signals or barrier semaphores. Data moves between devices by JAX's collectives and lax.ppermute only.
A program may use at most 64 MiB of HBM per device.

```python
import math
import jax
import jax.numpy as jnp
from jax import lax

SERIES = 16384
FACTORS = 512
INTERVAL_COUNT = 4096


def draw_persistence(key, part):
    key = jax.random.fold_in(key, 11)
    lowest = math.log(0.3 / INTERVAL_COUNT)
    highest = math.log(0.08)
    rates = jnp.exp(jax.random.uniform(key, (FACTORS,), jnp.float32, lowest, highest))
    return 1.0 - rates


def draw_factor_noise(key, part):
    key = jax.random.fold_in(key, 23)
    first, latter_piece, third, quartic_moment = jax.random.split(key, 4)
    lowest = math.log(1e-09)
    highest = math.log(0.3)
    floor_value = jnp.exp(jax.random.uniform(first, (1, FACTORS), jnp.float32, lowest, highest))
    spike_interval_width = jax.random.randint(latter_piece, (INTERVAL_COUNT, 1), 0, INTERVAL_COUNT) < 3
    raise_offset = jnp.exp(jax.random.uniform(third, (INTERVAL_COUNT, FACTORS), jnp.float32, math.log(30.0), math.log(300.0)))
    jagged_disturbance = jnp.exp(jax.random.uniform(quartic_moment, (INTERVAL_COUNT, FACTORS), jnp.float32, -0.5, 0.5))
    return floor_value * jnp.where(spike_interval_width, raise_offset, 1.0) * jagged_disturbance


def with_ends(values, stream_key, low, top_value):
    longest = values.shape.index(max(values.shape))
    spots = []
    for shift in (0, 1):
        where = [jax.random.randint(jax.random.fold_in(stream_key, axis), (), 0, length) for axis, length in enumerate(values.shape)]
        where[longest] = (where[longest] + shift) % values.shape[longest]
        spots.append(tuple(where))
    return values.at[spots[0]].set(low).at[spots[1]].set(top_value)


def shard_levels(rng, extent, shards, smallest, high):
    level = 1.0
    for position, blocks in shards:
        heights = jax.random.uniform(jax.random.fold_in(jax.random.fold_in(rng, 6), position), (blocks,), jnp.float32, smallest / len(shards), high / len(shards))
        level = level * jnp.repeat(jnp.exp(heights), extent[position] // blocks).reshape((-1,) + (1,) * (len(extent) - 1 - position))
    return level


def bell_draw(key, shape, spread, bound, shards=(), held_as=jnp.bfloat16):
    array = jax.random.normal(key, shape, jnp.float32) * spread
    if len(shards) > 0:
        array = shard_levels(key, shape, shards, -0.22, 0.18) * array
    return jnp.clip(array, min=-bound, max=bound).astype(held_as)


def setup_inputs(seed: int = 0) -> dict:
    streams_of = jax.random.split(jax.random.key(seed), 7)
    returns = bell_draw(streams_of[0], (INTERVAL_COUNT, SERIES), 1.0, 6.0, ((0, 64), (1, 8)), jnp.float32)
    variances = jnp.clip(jnp.exp(math.log(6.0) - 2.9957322 * jax.random.uniform(streams_of[1], (INTERVAL_COUNT, SERIES), jnp.float32) ** shard_levels(streams_of[1], (INTERVAL_COUNT, SERIES), ((0, 64), (1, 8)), -0.2, 0.2)), 0.3, 6.0)
    loadings = bell_draw(streams_of[2], (SERIES,), 1.0, 4.0, ((0, 8),), jnp.float32)
    sector = with_ends(jax.random.randint(streams_of[3], (SERIES,), 0, FACTORS), jax.random.fold_in(streams_of[3], 1), 0, FACTORS - 1).astype(jnp.int32)
    persistence = draw_persistence(jax.random.fold_in(streams_of[6], 71), 0)
    factor_noise = draw_factor_noise(jax.random.fold_in(streams_of[6], 71), 0)
    return {"returns": returns, "variances": variances, "loadings": loadings, "sector": sector, "persistence": persistence, "factor_noise": factor_noise}


def reference(returns, variances, loadings, sector, persistence, factor_noise):
    weights = 1.0 / variances
    signal = jax.ops.segment_sum((returns * weights * loadings[None, :]).T, sector, num_segments=FACTORS).T
    information = jax.ops.segment_sum((weights * (loadings * loadings)[None, :]).T, sector, num_segments=FACTORS).T

    def forward(carry, inputs):
        mean_prev, cov_prev = carry
        signal_bar, info_bar, noise_bar = inputs
        predicted = persistence * persistence * cov_prev + noise_bar
        inverse = 1.0 / (1.0 + predicted * info_bar)
        mean_now = (persistence * mean_prev + predicted * signal_bar) * inverse
        cov_now = predicted * inverse
        return (mean_now, cov_now), (mean_now, cov_now)

    zeros = jnp.zeros((FACTORS,), jnp.float32)
    unused_carry, (filt_mean, filt_cov) = lax.scan(forward, (zeros, zeros), (signal, information, factor_noise))

    def backward(carry, inputs):
        mean_next, var_next = carry
        mean_bar, cov_bar, noise_next = inputs
        ahead = persistence * persistence * cov_bar + noise_next
        smooth_gain = persistence * cov_bar / ahead
        remain = noise_next / ahead
        mean_now = smooth_gain * mean_next + remain * mean_bar
        var_now = smooth_gain * smooth_gain * var_next + remain * cov_bar
        return (mean_now, var_now), (mean_now, var_now)

    start_pair = (filt_mean[-1], filt_cov[-1])
    unused_last, (means_back, vars_back) = lax.scan(backward, start_pair, (filt_mean[:-1], filt_cov[:-1], factor_noise[1:]), reverse=True)
    smoothed_mean = jnp.concatenate([means_back, filt_mean[-1:]], axis=0)
    smoothed_var = jnp.concatenate([vars_back, filt_cov[-1:]], axis=0)
    return smoothed_mean, jnp.log(smoothed_var)
```

```python
import functools

import jax
import jax.numpy as jnp
from jax import lax
from jax.experimental import pallas as pl
from jax.experimental.pallas import tpu as pltpu
from jax.sharding import PartitionSpec as P

SUB = 8
LANES = 128
HALF = 64


def combine(earlier, later):
    left_gain, left_mean, left_cov, left_info, left_prec = earlier
    right_gain, right_mean, right_cov, right_info, right_prec = later
    inverse = 1.0 / (1.0 + left_cov * right_prec)
    right_scaled = right_gain * inverse
    left_scaled = left_gain * inverse
    return (
        right_scaled * left_gain,
        right_scaled * (left_mean + left_cov * right_info) + right_mean,
        right_scaled * right_gain * left_cov + right_cov,
        left_scaled * (right_info - right_prec * left_mean) + left_info,
        left_scaled * left_gain * right_prec + left_prec,
    )


def keep(mask, element):
    return tuple(jnp.where(mask, part, fill) for part, fill in zip(element, (1.0, 0.0, 0.0, 0.0, 0.0)))


def rolled(element, shift, axis):
    return tuple(pltpu.roll(part, shift, axis) for part in element)


def iotas():
    lane = lax.broadcasted_iota(jnp.int32, (SUB, LANES), 1)
    sub = lax.broadcasted_iota(jnp.int32, (SUB, LANES), 0)
    return lane, sub


def project_kernel(returns_ref, variances_ref, loadings_ref, sector_ref, out_ref):
    bars, series = returns_ref.shape
    peers = out_ref.shape[0]
    factors = peers * HALF
    loadings = loadings_ref[...]
    scaled = loadings / variances_ref[...]
    stacked = jnp.concatenate([returns_ref[...] * scaled, scaled * loadings], axis=0)
    upper = stacked.astype(jnp.bfloat16)
    lower = (stacked - upper.astype(jnp.float32)).astype(jnp.bfloat16)
    owner = lax.broadcasted_iota(jnp.int32, (factors, series), 0)
    one_hot = jnp.where(owner == sector_ref[...], 1.0, 0.0).astype(jnp.bfloat16)
    both = lax.dot_general(
        jnp.concatenate([upper, lower], axis=0),
        one_hot,
        (((1,), (1,)), ((), ())),
        preferred_element_type=jnp.float32,
    )
    total = both[: 2 * bars] + both[2 * bars :]
    half = bars // 2
    low_lanes = lax.broadcasted_iota(jnp.int32, (half, LANES), 1) < HALF
    for pair in range(factors // LANES):
        columns = slice(pair * LANES, (pair + 1) * LANES)
        for kind in range(2):
            first = total[kind * bars : kind * bars + half, columns]
            second = total[kind * bars + half : (kind + 1) * bars, columns]
            rows = slice(kind * half, (kind + 1) * half)
            out_ref[2 * pair, rows, :] = jnp.where(low_lanes, first, pltpu.roll(second, HALF, 1))
            out_ref[2 * pair + 1, rows, :] = jnp.where(low_lanes, pltpu.roll(first, HALF, 1), second)


def block_kernel(parts_ref, noise_ref, decay_ref, local_ref, summary_ref):
    peers, rows, _ = parts_ref.shape
    half = rows // 2
    depth = half // SUB
    lane, sub = iotas()
    decay = decay_ref[...]
    elements = []
    for step in range(depth):
        signal = parts_ref[0, pl.ds(step, SUB, stride=depth), :]
        information = parts_ref[0, pl.ds(half + step, SUB, stride=depth), :]
        for peer in range(1, peers):
            signal += parts_ref[peer, pl.ds(step, SUB, stride=depth), :]
            information += parts_ref[peer, pl.ds(half + step, SUB, stride=depth), :]
        noise = noise_ref[pl.ds(step, SUB, stride=depth), :]
        inverse = 1.0 / (1.0 + noise * information)
        decayed = decay * inverse
        scaled = noise * inverse
        elements.append((decayed, scaled * signal, scaled, decayed * signal, decay * decayed * information))
    forward = [elements[0]]
    for step in range(1, depth):
        forward.append(combine(forward[-1], elements[step]))
    backward = [None] * depth
    running = elements[-1]
    for step in range(depth - 2, -1, -1):
        backward[step] = running
        running = combine(elements[step], running)
    total = forward[-1]
    ahead, behind = total, total
    for shift in (1, 2, 4):
        ahead = combine(keep(sub >= shift, rolled(ahead, shift, 0)), ahead)
        behind = combine(behind, keep(sub < SUB - shift, rolled(behind, SUB - shift, 0)))
    other = tuple(
        jnp.broadcast_to(pltpu.roll(part[SUB - 1 :, :], HALF, 1), (SUB, LANES)) for part in ahead
    )
    before = combine(keep(lane >= HALF, other), keep(sub >= 1, rolled(ahead, 1, 0)))
    after = combine(keep(sub < SUB - 1, rolled(behind, SUB - 1, 0)), keep(lane < HALF, other))
    whole = combine(other, ahead)
    turned = rolled(whole, HALF, 1)
    rows_out = (
        jnp.where(lane < HALF, turned[0], whole[1]),
        jnp.where(lane < HALF, turned[2], whole[3]),
        jnp.where(lane < HALF, turned[4], whole[4]),
    )
    for row in range(3):
        summary_ref[row : row + 1, :] = rows_out[row][SUB - 1 :, :]
    summary_ref[3:4, :] = rows_out[2][SUB - 1 :, :]
    slot = 0
    for element in (before, after, *forward, *backward[:-1]):
        for part in element:
            local_ref[slot] = part
            slot += 1


def finish_kernel(place_ref, local_ref, gathered_ref, mean_ref, log_ref):
    blocks = gathered_ref.shape[0] // 4
    depth = (local_ref.shape[0] // 5 - 1) // 2
    strip = blocks // SUB
    mine = place_ref[0]
    lane, sub = iotas()
    low = lane < HALF
    pieces = []
    for step in range(strip):
        raw = [gathered_ref[pl.ds(4 * step + kind, SUB, stride=4 * strip), :] for kind in range(3)]
        turn = [pltpu.roll(part, HALF, 1) for part in raw[:2]]
        element = (
            jnp.where(low, raw[0], turn[0]),
            jnp.where(low, turn[0], raw[0]),
            jnp.where(low, raw[1], turn[1]),
            jnp.where(low, turn[1], raw[1]),
            raw[2],
        )
        block = sub * strip + step
        pieces.append(keep(jnp.where(low, block - mine, mine - block) < 0, element))
    while len(pieces) > 1:
        pieces = [combine(pieces[i], pieces[i + 1]) for i in range(0, len(pieces), 2)]
    total = pieces[0]
    for shift in (1, 2, 4):
        total = combine(total, rolled(total, SUB - shift, 0))
    own = [part[:1, :] for part in total]
    turn = [pltpu.roll(part, HALF, 1) for part in own]
    low_row = low[:1, :]
    mean_in = jnp.where(low_row, own[1], turn[1])
    cov_in = jnp.where(low_row, own[2], turn[2])
    info_in = jnp.where(low_row, turn[3], own[3])
    prec_in = jnp.where(low_row, turn[4], own[4])

    def element_at(index):
        return tuple(local_ref[5 * index + part] for part in range(5))

    def push(mean, cov, element):
        gain, shift_mean, shift_cov, info, prec = element
        scaled = gain / (1.0 + cov * prec)
        return scaled * (mean + cov * info) + shift_mean, scaled * gain * cov + shift_cov

    def pull(info, prec, element):
        gain, shift_mean, shift_cov, own_info, own_prec = element
        scaled = gain / (1.0 + shift_cov * prec)
        return scaled * (info - prec * shift_mean) + own_info, scaled * gain * prec + own_prec

    mean_in, cov_in = push(mean_in, cov_in, element_at(0))
    info_in, prec_in = pull(info_in, prec_in, element_at(1))
    for step in range(depth):
        mean, cov = push(mean_in, cov_in, element_at(2 + step))
        if step < depth - 1:
            info, prec = pull(info_in, prec_in, element_at(2 + depth + step))
        else:
            info, prec = info_in, prec_in
        inverse = 1.0 / (1.0 + cov * prec)
        smoothed = (mean + cov * info) * inverse
        logged = jnp.log(cov * inverse)
        for ref, value in ((mean_ref, smoothed), (log_ref, logged)):
            ref[pl.ds(step, SUB, stride=depth), :] = value[:, :HALF]
            ref[pl.ds(SUB * depth + step, SUB, stride=depth), :] = pltpu.roll(value, HALF, 1)[:, :HALF]


VMEM = pl.BlockSpec(memory_space=pltpu.VMEM)
SMEM = pl.BlockSpec(memory_space=pltpu.SMEM)


def body(returns, variances, loadings, sector, persistence, factor_noise):
    bars, series = returns.shape
    peers = lax.axis_size("rows")
    blocks = lax.axis_size("tm")
    half = bars // 2
    depth = half // SUB
    count = 2 * depth + 1
    sends = pl.pallas_call(
        project_kernel,
        out_shape=jax.ShapeDtypeStruct((peers, bars, LANES), jnp.float32),
        in_specs=[VMEM] * 4,
        out_specs=VMEM,
        compiler_params=pltpu.CompilerParams(vmem_limit_bytes=32 * 1024 * 1024),
    )(returns, variances, loadings[None, :], sector[None, :])
    offset = lax.axis_index("rows") * HALF
    noise = lax.dynamic_slice_in_dim(factor_noise, offset, HALF, 1)
    noise = jnp.concatenate([noise[:half], noise[half:]], axis=1)
    decay = lax.dynamic_slice_in_dim(persistence, offset, HALF, 0)
    decay = jnp.concatenate([decay, decay])[None, :]
    parts = lax.all_to_all(sends, "rows", 0, 0)
    local, summary = pl.pallas_call(
        block_kernel,
        out_shape=(
            jax.ShapeDtypeStruct((5 * count, SUB, LANES), jnp.float32),
            jax.ShapeDtypeStruct((4, LANES), jnp.float32),
        ),
        in_specs=[VMEM] * 3,
        out_specs=(VMEM, VMEM),
    )(parts, noise, decay)
    spread = jnp.broadcast_to(summary[None], (blocks, 4, LANES))
    gathered = lax.all_to_all(spread, "tm", 0, 0)
    place = jnp.reshape(lax.axis_index("tm"), (1,)).astype(jnp.int32)
    return pl.pallas_call(
        finish_kernel,
        out_shape=(
            jax.ShapeDtypeStruct((bars, HALF), jnp.float32),
            jax.ShapeDtypeStruct((bars, HALF), jnp.float32),
        ),
        in_specs=[SMEM, VMEM, VMEM],
        out_specs=(VMEM, VMEM),
    )(place, local, gathered.reshape(blocks * 4, LANES))


def solution(mesh):
    in_specs = (P("tm", "rows"), P("tm", "rows"), P("rows"), P("rows"), P(), P("tm", None))
    out_specs = (P("tm", "rows"), P("tm", "rows"))
    return jax.shard_map(body, mesh=mesh, in_specs=in_specs, out_specs=out_specs, check_vma=False)
```

```python
import functools

import jax
import jax.numpy as jnp
from jax import lax
from jax.experimental import pallas as pl
from jax.experimental.pallas import tpu as pltpu
from jax.sharding import Mesh, PartitionSpec as P

SUB = 8
LANES = 128
HALF = 64


def combine(earlier, later):
    left_gain, left_mean, left_cov, left_info, left_prec = earlier
    right_gain, right_mean, right_cov, right_info, right_prec = later
    inverse = 1.0 / (1.0 + left_cov * right_prec)
    right_scaled = right_gain * inverse
    left_scaled = left_gain * inverse
    return (
        right_scaled * left_gain,
        right_scaled * (left_mean + left_cov * right_info) + right_mean,
        right_scaled * right_gain * left_cov + right_cov,
        left_scaled * (right_info - right_prec * left_mean) + left_info,
        left_scaled * left_gain * right_prec + left_prec,
    )


def keep(mask, element):
    return tuple(jnp.where(mask, part, fill) for part, fill in zip(element, (1.0, 0.0, 0.0, 0.0, 0.0)))


def rolled(element, shift, axis):
    return tuple(pltpu.roll(part, shift, axis) for part in element)


def iotas():
    lane = lax.broadcasted_iota(jnp.int32, (SUB, LANES), 1)
    sub = lax.broadcasted_iota(jnp.int32, (SUB, LANES), 0)
    return lane, sub


def project_kernel(
    returns_hbm, variances_hbm, loadings_hbm, sector_hbm, out_ref,
    returns_ref, variances_ref, loadings_ref, sector_ref, sems,
):
    bars, series = returns_ref.shape
    peers = out_ref.shape[0]
    factors = peers * HALF
    copies = [
        pltpu.make_async_copy(source, target, sems.at[index])
        for index, (source, target) in enumerate(
            (
                (sector_hbm, sector_ref),
                (loadings_hbm, loadings_ref),
                (variances_hbm, variances_ref),
                (returns_hbm, returns_ref),
            )
        )
    ]
    for copy in copies:
        copy.start()
    copies[0].wait()
    owner = lax.broadcasted_iota(jnp.int32, (factors, series), 0)
    one_hot = jnp.where(owner == sector_ref[...], 1.0, 0.0).astype(jnp.bfloat16)
    for copy in copies[1:]:
        copy.wait()
    loadings = loadings_ref[...]
    scaled = loadings / variances_ref[...]
    stacked = jnp.concatenate([returns_ref[...] * scaled, scaled * loadings], axis=0)
    upper = stacked.astype(jnp.bfloat16)
    lower = (stacked - upper.astype(jnp.float32)).astype(jnp.bfloat16)
    both = lax.dot_general(
        jnp.concatenate([upper, lower], axis=0),
        one_hot,
        (((1,), (1,)), ((), ())),
        preferred_element_type=jnp.float32,
    )
    total = both[: 2 * bars] + both[2 * bars :]
    half = bars // 2
    low_lanes = lax.broadcasted_iota(jnp.int32, (half, LANES), 1) < HALF
    for pair in range(factors // LANES):
        columns = slice(pair * LANES, (pair + 1) * LANES)
        for kind in range(2):
            first = total[kind * bars : kind * bars + half, columns]
            second = total[kind * bars + half : (kind + 1) * bars, columns]
            rows = slice(kind * half, (kind + 1) * half)
            out_ref[2 * pair, rows, :] = jnp.where(low_lanes, first, pltpu.roll(second, HALF, 1))
            out_ref[2 * pair + 1, rows, :] = jnp.where(low_lanes, pltpu.roll(first, HALF, 1), second)


def added(terms):
    while len(terms) > 1:
        terms = [sum(terms[i + 1 : i + 2], terms[i]) for i in range(0, len(terms), 2)]
    return terms[0]


def spread(ref, rows):
    tile = jnp.concatenate([*rows, jnp.zeros((SUB - 5, LANES), jnp.float32)], axis=0)
    for peer in range(ref.shape[0]):
        ref[peer] = tile


def block_kernel(parts_ref, noise_ref, decay_ref, local_ref, summary_ref):
    peers, rows, _ = parts_ref.shape
    half = rows // 2
    depth = half // SUB
    lane, sub = iotas()
    decay = decay_ref[...]
    elements = []
    for step in range(depth):
        signal = added([parts_ref[peer, pl.ds(step, SUB, stride=depth), :] for peer in range(peers)])
        information = added(
            [parts_ref[peer, pl.ds(half + step, SUB, stride=depth), :] for peer in range(peers)]
        )
        noise = noise_ref[pl.ds(step, SUB, stride=depth), :]
        inverse = 1.0 / (1.0 + noise * information)
        decayed = decay * inverse
        scaled = noise * inverse
        elements.append((decayed, scaled * signal, scaled, decayed * signal, decay * decayed * information))
    forward = [elements[0]]
    for step in range(1, depth):
        forward.append(combine(forward[-1], elements[step]))
    backward = [None] * depth
    running = elements[-1]
    for step in range(depth - 2, -1, -1):
        backward[step] = running
        running = combine(elements[step], running)
    total = forward[-1]
    ahead, behind = total, total
    for shift in (1, 2, 4):
        ahead = combine(keep(sub >= shift, rolled(ahead, shift, 0)), ahead)
        behind = combine(behind, keep(sub < SUB - shift, rolled(behind, SUB - shift, 0)))
    other = tuple(
        jnp.broadcast_to(pltpu.roll(part[SUB - 1 :, :], HALF, 1), (SUB, LANES)) for part in ahead
    )
    before = combine(keep(lane >= HALF, other), keep(sub >= 1, rolled(ahead, 1, 0)))
    after = combine(keep(sub < SUB - 1, rolled(behind, SUB - 1, 0)), keep(lane < HALF, other))
    whole = combine(other, ahead)
    high = lane[:1, :] >= HALF
    rows = [part[SUB - 1 :, :] for part in whole]
    spread(summary_ref, [jnp.where(high, row, pltpu.roll(row, HALF, 1)) for row in rows])
    slot = 0
    for element in (before, after, *forward, *backward[:-1]):
        for part in element:
            local_ref[slot] = part
            slot += 1


def read_rows(ref):
    return tuple(ref[part : part + 1, :] for part in range(5))


def swapped(element, low):
    mask = lax.broadcasted_iota(jnp.int32, (1, LANES), 1) < HALF
    turn = rolled(element, HALF, 1)
    return tuple(
        jnp.where(mask, own, other) if low else jnp.where(mask, other, own) for own, other in zip(element, turn)
    )


def product(element):
    for shift in (1, 2, 4):
        element = combine(element, rolled(element, SUB - shift, 0))
    return tuple(part[:1, :] for part in element)


def received_rows(ref):
    return tuple(ref[pl.ds(part, SUB, stride=SUB), :] for part in range(5))


def around(place, received):
    lane, sub = iotas()
    return product(keep(jnp.where(lane < HALF, sub - place, place - sub) < 0, received))


def extended(inner, outer):
    mask = lax.broadcasted_iota(jnp.int32, (1, LANES), 1) < HALF
    earlier = tuple(jnp.where(mask, o, i) for i, o in zip(inner, outer))
    later = tuple(jnp.where(mask, i, o) for i, o in zip(inner, outer))
    return combine(earlier, later)


def level_kernel(received_ref, context_ref, total_ref):
    place = lax.axis_index("near")
    received = received_rows(received_ref)
    for part, row in enumerate(around(place, received)):
        context_ref[part : part + 1, :] = row
    context_ref[5:, :] = jnp.zeros((SUB - 5, LANES), jnp.float32)
    spread(total_ref, product(received))


def finish_kernel(local_ref, context_ref, received_ref, mean_ref, log_ref):
    depth = (local_ref.shape[0] // 5 - 1) // 2
    place = lax.axis_index("far")
    total = extended(read_rows(context_ref), around(place, received_rows(received_ref)))
    before, after = swapped(total, True), swapped(total, False)
    mean_in, cov_in = before[1], before[2]
    info_in, prec_in = after[3], after[4]

    def element_at(index):
        return tuple(local_ref[5 * index + part] for part in range(5))

    def push(mean, cov, element):
        gain, shift_mean, shift_cov, info, prec = element
        scaled = gain / (1.0 + cov * prec)
        return scaled * (mean + cov * info) + shift_mean, scaled * gain * cov + shift_cov

    def pull(info, prec, element):
        gain, shift_mean, shift_cov, own_info, own_prec = element
        scaled = gain / (1.0 + shift_cov * prec)
        return scaled * (info - prec * shift_mean) + own_info, scaled * gain * prec + own_prec

    mean_in, cov_in = push(mean_in, cov_in, element_at(0))
    info_in, prec_in = pull(info_in, prec_in, element_at(1))
    for step in range(depth):
        mean, cov = push(mean_in, cov_in, element_at(2 + step))
        if step < depth - 1:
            info, prec = pull(info_in, prec_in, element_at(2 + depth + step))
        else:
            info, prec = info_in, prec_in
        inverse = 1.0 / (1.0 + cov * prec)
        smoothed = (mean + cov * info) * inverse
        logged = jnp.log(cov * inverse)
        for ref, value in ((mean_ref, smoothed), (log_ref, logged)):
            ref[pl.ds(step, SUB, stride=depth), :] = value[:, :HALF]
            ref[pl.ds(SUB * depth + step, SUB, stride=depth), :] = pltpu.roll(value, HALF, 1)[:, :HALF]


VMEM = pl.BlockSpec(memory_space=pltpu.VMEM)


SMALL = pltpu.CompilerParams(vmem_limit_bytes=4 * 1024 * 1024)


def body(returns, variances, loadings, sector, persistence, factor_noise):
    bars, series = returns.shape
    peers = lax.axis_size("rows")
    half = bars // 2
    depth = half // SUB
    count = 2 * depth + 1
    row = lax.axis_index("rows")
    tile = jax.ShapeDtypeStruct((SUB, LANES), jnp.float32)
    tiles = jax.ShapeDtypeStruct((SUB, SUB, LANES), jnp.float32)
    sends = pl.pallas_call(
        project_kernel,
        out_shape=jax.ShapeDtypeStruct((peers, bars, LANES), jnp.float32),
        in_specs=[pl.BlockSpec(memory_space=pl.ANY)] * 4,
        out_specs=VMEM,
        scratch_shapes=[
            pltpu.VMEM((bars, series), jnp.float32),
            pltpu.VMEM((bars, series), jnp.float32),
            pltpu.VMEM((1, series), jnp.float32),
            pltpu.VMEM((1, series), jnp.int32),
            pltpu.SemaphoreType.DMA((4,)),
        ],
    )(returns, variances, loadings[None, :], sector[None, :])
    parts = lax.all_to_all(sends, "rows", 0, 0)
    offset = row * HALF
    noise = lax.dynamic_slice_in_dim(factor_noise, offset, HALF, 1)
    noise = jnp.concatenate([noise[:half], noise[half:]], axis=1)
    decay = lax.dynamic_slice_in_dim(persistence, offset, HALF, 0)
    decay = jnp.concatenate([decay, decay])[None, :]
    local, totals = pl.pallas_call(
        block_kernel,
        out_shape=(jax.ShapeDtypeStruct((5 * count, SUB, LANES), jnp.float32), tiles),
        in_specs=[VMEM] * 3,
        out_specs=(VMEM, VMEM),
        compiler_params=SMALL,
    )(parts, noise, decay)
    received = lax.all_to_all(totals, "near", 0, 0)
    context, totals = pl.pallas_call(
        level_kernel,
        out_shape=(tile, tiles),
        in_specs=[VMEM],
        out_specs=(VMEM, VMEM),
        compiler_params=SMALL,
    )(received.reshape(SUB * SUB, LANES))
    received = lax.all_to_all(totals, "far", 0, 0)
    return pl.pallas_call(
        finish_kernel,
        out_shape=(
            jax.ShapeDtypeStruct((bars, HALF), jnp.float32),
            jax.ShapeDtypeStruct((bars, HALF), jnp.float32),
        ),
        in_specs=[VMEM] * 3,
        out_specs=(VMEM, VMEM),
        compiler_params=SMALL,
    )(local, context, received.reshape(SUB * SUB, LANES))


def solution(mesh):
    blocks, peers = mesh.shape["tm"], mesh.shape["rows"]
    split = Mesh(mesh.devices.reshape(blocks // SUB, SUB, peers), ("far", "near", "rows"))
    bars = ("far", "near")
    in_specs = (P(bars, "rows"), P(bars, "rows"), P("rows"), P("rows"), P(), P(bars, None))
    out_specs = (P(bars, "rows"), P(bars, "rows"))
    return jax.shard_map(body, mesh=split, in_specs=in_specs, out_specs=out_specs, check_vma=False)
```

```python
import functools

import jax
import jax.numpy as jnp
from jax import lax
from jax.experimental import pallas as pl
from jax.experimental.pallas import tpu as pltpu
from jax.sharding import PartitionSpec as P

SUB = 8
LANES = 128
HALF = 64
PIECE = 512


def combine(earlier, later):
    left_gain, left_mean, left_cov, left_info, left_prec = earlier
    right_gain, right_mean, right_cov, right_info, right_prec = later
    inverse = 1.0 / (1.0 + left_cov * right_prec)
    right_scaled = right_gain * inverse
    left_scaled = left_gain * inverse
    return (
        right_scaled * left_gain,
        right_scaled * (left_mean + left_cov * right_info) + right_mean,
        right_scaled * right_gain * left_cov + right_cov,
        left_scaled * (right_info - right_prec * left_mean) + left_info,
        left_scaled * left_gain * right_prec + left_prec,
    )


def keep(mask, element):
    return tuple(jnp.where(mask, part, fill) for part, fill in zip(element, (1.0, 0.0, 0.0, 0.0, 0.0)))


def rolled(element, shift, axis):
    return tuple(pltpu.roll(part, shift, axis) for part in element)


def iotas():
    lane = lax.broadcasted_iota(jnp.int32, (SUB, LANES), 1)
    sub = lax.broadcasted_iota(jnp.int32, (SUB, LANES), 0)
    return lane, sub


def project_kernel(
    returns_hbm, variances_hbm, loadings_hbm, sector_hbm, noise_hbm, decay_hbm,
    out_ref, noise_out, decay_out,
    returns_ref, variances_ref, loadings_ref, sector_ref, noise_ref, decay_ref, sems,
):
    bars, series = returns_ref.shape
    peers = out_ref.shape[0]
    factors = peers * HALF
    pieces = [slice(first, first + PIECE) for first in range(0, series, PIECE)]
    moves = [(sector_hbm, sector_ref), (loadings_hbm, loadings_ref)]
    for piece in pieces:
        moves.append((variances_hbm.at[:, piece], variances_ref.at[:, piece]))
        moves.append((returns_hbm.at[:, piece], returns_ref.at[:, piece]))
    row = lax.axis_index("rows")
    columns = pl.ds(pl.multiple_of(row // 2 * LANES, LANES), LANES)
    moves.append((noise_hbm.at[:, columns], noise_ref))
    moves.append((decay_hbm.at[:, columns], decay_ref))
    copies = [pltpu.make_async_copy(*move, sems.at[index]) for index, move in enumerate(moves)]
    for copy in copies:
        copy.start()
    copies[0].wait()
    owner = lax.broadcasted_iota(jnp.int32, (factors, PIECE), 0)
    one_hot = [
        jnp.where(owner == sector_ref[:, piece], 1.0, 0.0).astype(jnp.bfloat16) for piece in pieces
    ]
    copies[1].wait()
    both = jnp.zeros((4 * bars, factors), jnp.float32)
    for index, piece in enumerate(pieces):
        copies[2 + 2 * index].wait()
        copies[3 + 2 * index].wait()
        loadings = loadings_ref[:, piece]
        scaled = loadings / variances_ref[:, piece]
        stacked = jnp.concatenate([returns_ref[:, piece] * scaled, scaled * loadings], axis=0)
        upper = stacked.astype(jnp.bfloat16)
        lower = (stacked - upper.astype(jnp.float32)).astype(jnp.bfloat16)
        both += lax.dot_general(
            jnp.concatenate([upper, lower], axis=0),
            one_hot[index],
            (((1,), (1,)), ((), ())),
            preferred_element_type=jnp.float32,
        )
    total = both[: 2 * bars] + both[2 * bars :]
    half = bars // 2
    low_lanes = lax.broadcasted_iota(jnp.int32, (half, LANES), 1) < HALF
    copies[-2].wait()
    copies[-1].wait()
    upper_half = jnp.full((half, LANES), row % 2, jnp.int32) == 1
    early, late = noise_ref[:half, :], noise_ref[half:, :]
    noise_out[...] = jnp.where(
        low_lanes,
        jnp.where(upper_half, pltpu.roll(early, HALF, 1), early),
        jnp.where(upper_half, late, pltpu.roll(late, HALF, 1)),
    )
    decay = decay_ref[...]
    decay_out[...] = jnp.where(low_lanes[:1] == upper_half[:1], pltpu.roll(decay, HALF, 1), decay)
    for pair in range(factors // LANES):
        columns = slice(pair * LANES, (pair + 1) * LANES)
        for kind in range(2):
            first = total[kind * bars : kind * bars + half, columns]
            second = total[kind * bars + half : (kind + 1) * bars, columns]
            rows = slice(kind * half, (kind + 1) * half)
            out_ref[2 * pair, rows, :] = jnp.where(low_lanes, first, pltpu.roll(second, HALF, 1))
            out_ref[2 * pair + 1, rows, :] = jnp.where(low_lanes, pltpu.roll(first, HALF, 1), second)


def added(terms):
    while len(terms) > 1:
        terms = [sum(terms[i + 1 : i + 2], terms[i]) for i in range(0, len(terms), 2)]
    return terms[0]


def block_kernel(parts_ref, noise_ref, decay_ref, local_ref, summary_hbm, summary_ref, sem):
    peers, rows, _ = parts_ref.shape
    half = rows // 2
    depth = half // SUB
    lane, sub = iotas()
    decay = decay_ref[...]
    elements = []
    for step in range(depth):
        signal = added([parts_ref[peer, pl.ds(step, SUB, stride=depth), :] for peer in range(peers)])
        information = added(
            [parts_ref[peer, pl.ds(half + step, SUB, stride=depth), :] for peer in range(peers)]
        )
        noise = noise_ref[pl.ds(step, SUB, stride=depth), :]
        inverse = 1.0 / (1.0 + noise * information)
        decayed = decay * inverse
        scaled = noise * inverse
        elements.append((decayed, scaled * signal, scaled, decayed * signal, decay * decayed * information))
    forward = [elements[0]]
    for step in range(1, depth):
        forward.append(combine(forward[-1], elements[step]))
    backward = [None] * depth
    running = elements[-1]
    for step in range(depth - 2, -1, -1):
        backward[step] = running
        running = combine(elements[step], running)
    total = forward[-1]
    ahead, behind = total, total
    for shift in (1, 2, 4):
        ahead = combine(keep(sub >= shift, rolled(ahead, shift, 0)), ahead)
        behind = combine(behind, keep(sub < SUB - shift, rolled(behind, SUB - shift, 0)))
    other = tuple(
        jnp.broadcast_to(pltpu.roll(part[SUB - 1 :, :], HALF, 1), (SUB, LANES)) for part in ahead
    )
    before = combine(keep(lane >= HALF, other), keep(sub >= 1, rolled(ahead, 1, 0)))
    after = combine(keep(sub < SUB - 1, rolled(behind, SUB - 1, 0)), keep(lane < HALF, other))
    whole = combine(other, ahead)
    low = lane[:1, :] < HALF
    rows = [part[SUB - 1 :, :] for part in whole]
    turned = [pltpu.roll(row, HALF, 1) for row in rows]
    packed = jnp.concatenate(
        [
            jnp.where(low, turned[0], rows[1]),
            jnp.where(low, turned[2], rows[3]),
            jnp.where(low, turned[4], rows[4]),
            jnp.zeros((1, LANES), jnp.float32),
        ],
        axis=0,
    )
    for peer in range(summary_ref.shape[0]):
        summary_ref[peer] = packed
    copy = pltpu.make_async_copy(summary_ref, summary_hbm, sem)
    copy.start()
    slot = 0
    for element in (before, after, *forward, *backward[:-1]):
        for part in element:
            local_ref[slot] = part
            slot += 1
    copy.wait()


def swapped(element, low):
    mask = lax.broadcasted_iota(jnp.int32, (1, LANES), 1) < HALF
    turn = rolled(element, HALF, 1)
    return tuple(
        jnp.where(mask, own, other) if low else jnp.where(mask, other, own) for own, other in zip(element, turn)
    )


def product(element):
    for shift in (1, 2, 4):
        element = combine(element, rolled(element, SUB - shift, 0))
    return tuple(part[:1, :] for part in element)


def finish_kernel(local_ref, received_ref, mean_ref, log_ref):
    depth = (local_ref.shape[0] // 5 - 1) // 2
    place = lax.axis_index("tm")
    lane, sub = iotas()
    low = lane < HALF
    strip = received_ref.shape[0] // (4 * SUB)
    pieces = []
    for step in range(strip):
        raw = [received_ref[pl.ds(4 * step + kind, SUB, stride=4 * strip), :] for kind in range(3)]
        turn = [pltpu.roll(part, HALF, 1) for part in raw[:2]]
        element = (
            jnp.where(low, raw[0], turn[0]),
            jnp.where(low, turn[0], raw[0]),
            jnp.where(low, raw[1], turn[1]),
            jnp.where(low, turn[1], raw[1]),
            raw[2],
        )
        block = sub * strip + step
        pieces.append(keep(jnp.where(low, block - place, place - block) < 0, element))
    while len(pieces) > 1:
        pieces = [combine(pieces[i], pieces[i + 1]) for i in range(0, len(pieces), 2)]
    total = product(pieces[0])
    before, after = swapped(total, True), swapped(total, False)
    mean_in, cov_in = before[1], before[2]
    info_in, prec_in = after[3], after[4]

    def element_at(index):
        return tuple(local_ref[5 * index + part] for part in range(5))

    def push(mean, cov, element):
        gain, shift_mean, shift_cov, info, prec = element
        scaled = gain / (1.0 + cov * prec)
        return scaled * (mean + cov * info) + shift_mean, scaled * gain * cov + shift_cov

    def pull(info, prec, element):
        gain, shift_mean, shift_cov, own_info, own_prec = element
        scaled = gain / (1.0 + shift_cov * prec)
        return scaled * (info - prec * shift_mean) + own_info, scaled * gain * prec + own_prec

    mean_in, cov_in = push(mean_in, cov_in, element_at(0))
    info_in, prec_in = pull(info_in, prec_in, element_at(1))
    for step in range(depth):
        mean, cov = push(mean_in, cov_in, element_at(2 + step))
        if step < depth - 1:
            info, prec = pull(info_in, prec_in, element_at(2 + depth + step))
        else:
            info, prec = info_in, prec_in
        inverse = 1.0 / (1.0 + cov * prec)
        smoothed = (mean + cov * info) * inverse
        logged = jnp.log(cov * inverse)
        for ref, value in ((mean_ref, smoothed), (log_ref, logged)):
            ref[pl.ds(step, SUB, stride=depth), :] = value[:, :HALF]
            ref[pl.ds(SUB * depth + step, SUB, stride=depth), :] = pltpu.roll(value, HALF, 1)[:, :HALF]


VMEM = pl.BlockSpec(memory_space=pltpu.VMEM)


SMALL = pltpu.CompilerParams(vmem_limit_bytes=4 * 1024 * 1024)


def body(returns, variances, loadings, sector, persistence, factor_noise):
    bars, series = returns.shape
    peers = lax.axis_size("rows")
    blocks = lax.axis_size("tm")
    half = bars // 2
    depth = half // SUB
    count = 2 * depth + 1
    inputs = [
        pltpu.with_memory_space_constraint(array, pltpu.HBM)
        for array in (
            returns, variances, loadings[None, :], sector[None, :], factor_noise, persistence[None, :]
        )
    ]
    sends, noise, decay = pl.pallas_call(
        project_kernel,
        out_shape=(
            pltpu.VMEM((peers, bars, LANES), jnp.float32),
            pltpu.VMEM((half, LANES), jnp.float32),
            pltpu.VMEM((1, LANES), jnp.float32),
        ),
        in_specs=[pl.BlockSpec(memory_space=pltpu.HBM)] * 6,
        out_specs=(VMEM, VMEM, VMEM),
        scratch_shapes=[
            pltpu.VMEM((bars, series), jnp.float32),
            pltpu.VMEM((bars, series), jnp.float32),
            pltpu.VMEM((1, series), jnp.float32),
            pltpu.VMEM((1, series), jnp.int32),
            pltpu.VMEM((bars, LANES), jnp.float32),
            pltpu.VMEM((1, LANES), jnp.float32),
            pltpu.SemaphoreType.DMA((4 + 2 * (series // PIECE),)),
        ],
        compiler_params=pltpu.CompilerParams(vmem_limit_bytes=24 * 1024 * 1024),
    )(*inputs)
    parts = lax.all_to_all(sends, "rows", 0, 0)
    local, summary = pl.pallas_call(
        block_kernel,
        out_shape=(
            jax.ShapeDtypeStruct((5 * count, SUB, LANES), jnp.float32),
            jax.ShapeDtypeStruct((blocks, 4, LANES), jnp.float32),
        ),
        in_specs=[VMEM] * 3,
        out_specs=(VMEM, pl.BlockSpec(memory_space=pltpu.HBM)),
        scratch_shapes=[pltpu.VMEM((blocks, 4, LANES), jnp.float32), pltpu.SemaphoreType.DMA],
        compiler_params=SMALL,
    )(parts, noise, decay)
    received = lax.all_to_all(summary, "tm", 0, 0)
    return pl.pallas_call(
        finish_kernel,
        out_shape=(
            jax.ShapeDtypeStruct((bars, HALF), jnp.float32),
            jax.ShapeDtypeStruct((bars, HALF), jnp.float32),
        ),
        in_specs=[VMEM] * 2,
        out_specs=(VMEM, VMEM),
        compiler_params=SMALL,
    )(local, received.reshape(blocks * 4, LANES))


def solution(mesh):
    in_specs = (P("tm", "rows"), P("tm", "rows"), P("rows"), P("rows"), P(), P("tm", None))
    out_specs = (P("tm", "rows"), P("tm", "rows"))
    return jax.shard_map(body, mesh=mesh, in_specs=in_specs, out_specs=out_specs, check_vma=False)
```

```python
import functools

import jax
import jax.numpy as jnp
from jax import lax
from jax.experimental import pallas as pl
from jax.experimental.pallas import tpu as pltpu
from jax.sharding import PartitionSpec as P

SUB = 8
LANES = 128
HALF = 64
PIECE = 1024
ROW_FIRST = 4
BLOCK_FIRST = 40


def combine(earlier, later):
    left_gain, left_mean, left_cov, left_info, left_prec = earlier
    right_gain, right_mean, right_cov, right_info, right_prec = later
    inverse = 1.0 / (1.0 + left_cov * right_prec)
    right_scaled = right_gain * inverse
    left_scaled = left_gain * inverse
    return (
        right_scaled * left_gain,
        right_scaled * (left_mean + left_cov * right_info) + right_mean,
        right_scaled * right_gain * left_cov + right_cov,
        left_scaled * (right_info - right_prec * left_mean) + left_info,
        left_scaled * left_gain * right_prec + left_prec,
    )


def keep(mask, element):
    return tuple(jnp.where(mask, part, fill) for part, fill in zip(element, (1.0, 0.0, 0.0, 0.0, 0.0)))


def rolled(element, shift, axis):
    return tuple(pltpu.roll(part, shift, axis) for part in element)


def iotas():
    lane = lax.broadcasted_iota(jnp.int32, (SUB, LANES), 1)
    sub = lax.broadcasted_iota(jnp.int32, (SUB, LANES), 0)
    return lane, sub


def project_kernel(
    returns_hbm, variances_hbm, loadings_hbm, sector_hbm, noise_hbm, decay_hbm,
    out_ref, noise_out, decay_out,
    returns_ref, variances_ref, loadings_ref, sector_ref, noise_ref, decay_ref, sems,
):
    bars, series = returns_ref.shape
    peers = out_ref.shape[0]
    factors = peers * HALF
    pieces = [slice(first, first + PIECE) for first in range(0, series, PIECE)]
    moves = [(sector_hbm, sector_ref), (loadings_hbm, loadings_ref)]
    for piece in pieces:
        moves.append((variances_hbm.at[:, piece], variances_ref.at[:, piece]))
        moves.append((returns_hbm.at[:, piece], returns_ref.at[:, piece]))
    row = lax.axis_index("rows")
    columns = pl.ds(pl.multiple_of(row // 2 * LANES, LANES), LANES)
    moves.append((noise_hbm.at[:, columns], noise_ref))
    moves.append((decay_hbm.at[:, columns], decay_ref))
    copies = [pltpu.make_async_copy(*move, sems.at[index]) for index, move in enumerate(moves)]
    for copy in copies:
        copy.start()
    copies[0].wait()
    owner = lax.broadcasted_iota(jnp.int32, (factors, PIECE), 0)
    one_hot = [
        jnp.where(owner == sector_ref[:, piece], 1.0, 0.0).astype(jnp.bfloat16) for piece in pieces
    ]
    copies[1].wait()
    both = jnp.zeros((4 * bars, factors), jnp.float32)
    for index, piece in enumerate(pieces):
        copies[2 + 2 * index].wait()
        copies[3 + 2 * index].wait()
        loadings = loadings_ref[:, piece]
        scaled = loadings / variances_ref[:, piece]
        stacked = jnp.concatenate([returns_ref[:, piece] * scaled, scaled * loadings], axis=0)
        upper = stacked.astype(jnp.bfloat16)
        lower = (stacked - upper.astype(jnp.float32)).astype(jnp.bfloat16)
        both += lax.dot_general(
            jnp.concatenate([upper, lower], axis=0),
            one_hot[index],
            (((1,), (1,)), ((), ())),
            preferred_element_type=jnp.float32,
        )
    total = both[: 2 * bars] + both[2 * bars :]
    half = bars // 2
    low_lanes = lax.broadcasted_iota(jnp.int32, (half, LANES), 1) < HALF
    copies[-2].wait()
    copies[-1].wait()
    upper_half = jnp.full((half, LANES), row % 2, jnp.int32) == 1
    early, late = noise_ref[:half, :], noise_ref[half:, :]
    noise_out[...] = jnp.where(
        low_lanes,
        jnp.where(upper_half, pltpu.roll(early, HALF, 1), early),
        jnp.where(upper_half, late, pltpu.roll(late, HALF, 1)),
    )
    decay = decay_ref[...]
    decay_out[...] = jnp.where(low_lanes[:1] == upper_half[:1], pltpu.roll(decay, HALF, 1), decay)
    for pair in range(factors // LANES):
        columns = slice(pair * LANES, (pair + 1) * LANES)
        for kind in range(2):
            first = total[kind * bars : kind * bars + half, columns]
            second = total[kind * bars + half : (kind + 1) * bars, columns]
            rows = slice(kind * half, (kind + 1) * half)
            first_slot = (2 * pair - ROW_FIRST) % peers
            out_ref[first_slot, rows, :] = jnp.where(low_lanes, first, pltpu.roll(second, HALF, 1))
            out_ref[(first_slot + 1) % peers, rows, :] = jnp.where(low_lanes, pltpu.roll(first, HALF, 1), second)


def added(terms):
    while len(terms) > 1:
        terms = [sum(terms[i + 1 : i + 2], terms[i]) for i in range(0, len(terms), 2)]
    return terms[0]


def block_kernel(parts_ref, noise_ref, decay_ref, local_ref, summary_hbm, summary_ref, sem):
    peers, rows, _ = parts_ref.shape
    half = rows // 2
    depth = half // SUB
    lane, sub = iotas()
    decay = decay_ref[...]
    elements = []
    for step in range(depth):
        signal = added([parts_ref[peer, pl.ds(step, SUB, stride=depth), :] for peer in range(peers)])
        information = added(
            [parts_ref[peer, pl.ds(half + step, SUB, stride=depth), :] for peer in range(peers)]
        )
        noise = noise_ref[pl.ds(step, SUB, stride=depth), :]
        inverse = 1.0 / (1.0 + noise * information)
        decayed = decay * inverse
        scaled = noise * inverse
        elements.append((decayed, scaled * signal, scaled, decayed * signal, decay * decayed * information))
    forward = [elements[0]]
    for step in range(1, depth):
        forward.append(combine(forward[-1], elements[step]))
    backward = [None] * depth
    running = elements[-1]
    for step in range(depth - 2, -1, -1):
        backward[step] = running
        running = combine(elements[step], running)
    total = forward[-1]
    ahead, behind = total, total
    for shift in (1, 2, 4):
        ahead = combine(keep(sub >= shift, rolled(ahead, shift, 0)), ahead)
        behind = combine(behind, keep(sub < SUB - shift, rolled(behind, SUB - shift, 0)))
    other = tuple(
        jnp.broadcast_to(pltpu.roll(part[SUB - 1 :, :], HALF, 1), (SUB, LANES)) for part in ahead
    )
    before = combine(keep(lane >= HALF, other), keep(sub >= 1, rolled(ahead, 1, 0)))
    after = combine(keep(sub < SUB - 1, rolled(behind, SUB - 1, 0)), keep(lane < HALF, other))
    whole = combine(other, ahead)
    low = lane[:1, :] < HALF
    rows = [part[SUB - 1 :, :] for part in whole]
    turned = [pltpu.roll(row, HALF, 1) for row in rows]
    packed = jnp.concatenate(
        [
            jnp.where(low, turned[0], rows[1]),
            jnp.where(low, turned[2], rows[3]),
            jnp.where(low, turned[4], rows[4]),
            jnp.zeros((1, LANES), jnp.float32),
        ],
        axis=0,
    )
    for peer in range(summary_ref.shape[0]):
        summary_ref[peer] = packed
    copy = pltpu.make_async_copy(summary_ref, summary_hbm, sem)
    copy.start()
    slot = 0
    for element in (before, after, *forward, *backward[:-1]):
        for part in element:
            local_ref[slot] = part
            slot += 1
    copy.wait()


def swapped(element, low):
    mask = lax.broadcasted_iota(jnp.int32, (1, LANES), 1) < HALF
    turn = rolled(element, HALF, 1)
    return tuple(
        jnp.where(mask, own, other) if low else jnp.where(mask, other, own) for own, other in zip(element, turn)
    )


def product(element):
    for shift in (1, 2, 4):
        element = combine(element, rolled(element, SUB - shift, 0))
    return tuple(part[:1, :] for part in element)


def finish_kernel(local_ref, received_ref, mean_ref, log_ref):
    depth = (local_ref.shape[0] // 5 - 1) // 2
    place = lax.axis_index("tm")
    lane, sub = iotas()
    low = lane < HALF
    strip = received_ref.shape[0] // (4 * SUB)
    pieces = []
    for step in range(strip):
        raw = [
            pltpu.roll(received_ref[pl.ds(4 * step + kind, SUB, stride=4 * strip), :], BLOCK_FIRST // SUB, 0)
            for kind in range(3)
        ]
        turn = [pltpu.roll(part, HALF, 1) for part in raw[:2]]
        element = (
            jnp.where(low, raw[0], turn[0]),
            jnp.where(low, turn[0], raw[0]),
            jnp.where(low, raw[1], turn[1]),
            jnp.where(low, turn[1], raw[1]),
            raw[2],
        )
        block = sub * strip + step
        pieces.append(keep(jnp.where(low, block - place, place - block) < 0, element))
    while len(pieces) > 1:
        pieces = [combine(pieces[i], pieces[i + 1]) for i in range(0, len(pieces), 2)]
    total = product(pieces[0])
    before, after = swapped(total, True), swapped(total, False)
    mean_in, cov_in = before[1], before[2]
    info_in, prec_in = after[3], after[4]

    def element_at(index):
        return tuple(local_ref[5 * index + part] for part in range(5))

    def push(mean, cov, element):
        gain, shift_mean, shift_cov, info, prec = element
        scaled = gain / (1.0 + cov * prec)
        return scaled * (mean + cov * info) + shift_mean, scaled * gain * cov + shift_cov

    def pull(info, prec, element):
        gain, shift_mean, shift_cov, own_info, own_prec = element
        scaled = gain / (1.0 + shift_cov * prec)
        return scaled * (info - prec * shift_mean) + own_info, scaled * gain * prec + own_prec

    mean_in, cov_in = push(mean_in, cov_in, element_at(0))
    info_in, prec_in = pull(info_in, prec_in, element_at(1))
    for step in range(depth):
        mean, cov = push(mean_in, cov_in, element_at(2 + step))
        if step < depth - 1:
            info, prec = pull(info_in, prec_in, element_at(2 + depth + step))
        else:
            info, prec = info_in, prec_in
        inverse = 1.0 / (1.0 + cov * prec)
        smoothed = (mean + cov * info) * inverse
        logged = jnp.log(cov * inverse)
        for ref, value in ((mean_ref, smoothed), (log_ref, logged)):
            ref[pl.ds(step, SUB, stride=depth), :] = value[:, :HALF]
            ref[pl.ds(SUB * depth + step, SUB, stride=depth), :] = pltpu.roll(value, HALF, 1)[:, :HALF]


VMEM = pl.BlockSpec(memory_space=pltpu.VMEM)


SMALL = pltpu.CompilerParams(vmem_limit_bytes=4 * 1024 * 1024)


def exchanged(x, axis, first):
    size = lax.axis_size(axis)
    return lax.all_to_all(x, axis, 0, 0, axis_index_groups=[[(first + i) % size for i in range(size)]])


def body(returns, variances, loadings, sector, persistence, factor_noise):
    bars, series = returns.shape
    peers = lax.axis_size("rows")
    blocks = lax.axis_size("tm")
    half = bars // 2
    depth = half // SUB
    count = 2 * depth + 1
    inputs = [
        pltpu.with_memory_space_constraint(array, pltpu.HBM)
        for array in (
            returns, variances, loadings[None, :], sector[None, :], factor_noise, persistence[None, :]
        )
    ]
    sends, noise, decay = pl.pallas_call(
        project_kernel,
        out_shape=(
            pltpu.VMEM((peers, bars, LANES), jnp.float32),
            pltpu.VMEM((half, LANES), jnp.float32),
            pltpu.VMEM((1, LANES), jnp.float32),
        ),
        in_specs=[pl.BlockSpec(memory_space=pltpu.HBM)] * 6,
        out_specs=(VMEM, VMEM, VMEM),
        scratch_shapes=[
            pltpu.VMEM((bars, series), jnp.float32),
            pltpu.VMEM((bars, series), jnp.float32),
            pltpu.VMEM((1, series), jnp.float32),
            pltpu.VMEM((1, series), jnp.int32),
            pltpu.VMEM((bars, LANES), jnp.float32),
            pltpu.VMEM((1, LANES), jnp.float32),
            pltpu.SemaphoreType.DMA((4 + 2 * (series // PIECE),)),
        ],
        compiler_params=pltpu.CompilerParams(vmem_limit_bytes=24 * 1024 * 1024),
    )(*inputs)
    parts = exchanged(sends, "rows", ROW_FIRST)
    local, summary = pl.pallas_call(
        block_kernel,
        out_shape=(
            jax.ShapeDtypeStruct((5 * count, SUB, LANES), jnp.float32),
            jax.ShapeDtypeStruct((blocks, 4, LANES), jnp.float32),
        ),
        in_specs=[VMEM] * 3,
        out_specs=(VMEM, pl.BlockSpec(memory_space=pltpu.HBM)),
        scratch_shapes=[pltpu.VMEM((blocks, 4, LANES), jnp.float32), pltpu.SemaphoreType.DMA],
        compiler_params=SMALL,
    )(parts, noise, decay)
    received = exchanged(summary, "tm", BLOCK_FIRST)
    return pl.pallas_call(
        finish_kernel,
        out_shape=(
            jax.ShapeDtypeStruct((bars, HALF), jnp.float32),
            jax.ShapeDtypeStruct((bars, HALF), jnp.float32),
        ),
        in_specs=[VMEM] * 2,
        out_specs=(VMEM, VMEM),
        compiler_params=SMALL,
    )(local, received.reshape(blocks * 4, LANES))


def solution(mesh):
    in_specs = (P("tm", "rows"), P("tm", "rows"), P("rows"), P("rows"), P(), P("tm", None))
    out_specs = (P("tm", "rows"), P("tm", "rows"))
    return jax.shard_map(body, mesh=mesh, in_specs=in_specs, out_specs=out_specs, check_vma=False)
```

```python
import functools

import jax
import jax.numpy as jnp
from jax import lax
from jax.experimental import pallas as pl
from jax.experimental.pallas import tpu as pltpu
from jax.sharding import PartitionSpec as P

SUB = 8
LANES = 128
HALF = 64
PIECE = 1024


def row_order(peers):
    first = peers // 2
    return sorted(range(peers), key=lambda y: (y != first, -min((y - first) % peers, (first - y) % peers), y))


def block_order(blocks):
    first = blocks * 23 // 32
    return [(first + i) % blocks for i in range(blocks)]


def combine(earlier, later):
    left_gain, left_mean, left_cov, left_info, left_prec = earlier
    right_gain, right_mean, right_cov, right_info, right_prec = later
    inverse = 1.0 / (1.0 + left_cov * right_prec)
    right_scaled = right_gain * inverse
    left_scaled = left_gain * inverse
    return (
        right_scaled * left_gain,
        right_scaled * (left_mean + left_cov * right_info) + right_mean,
        right_scaled * right_gain * left_cov + right_cov,
        left_scaled * (right_info - right_prec * left_mean) + left_info,
        left_scaled * left_gain * right_prec + left_prec,
    )


def keep(mask, element):
    return tuple(jnp.where(mask, part, fill) for part, fill in zip(element, (1.0, 0.0, 0.0, 0.0, 0.0)))


def rolled(element, shift, axis):
    return tuple(pltpu.roll(part, shift, axis) for part in element)


def iotas():
    lane = lax.broadcasted_iota(jnp.int32, (SUB, LANES), 1)
    sub = lax.broadcasted_iota(jnp.int32, (SUB, LANES), 0)
    return lane, sub


def project_kernel(
    returns_hbm, variances_hbm, loadings_hbm, sector_hbm, noise_hbm, decay_hbm,
    out_ref, noise_out, decay_out,
    returns_ref, variances_ref, loadings_ref, sector_ref, noise_ref, decay_ref, sems,
):
    bars, series = returns_ref.shape
    peers = out_ref.shape[0]
    factors = peers * HALF
    pieces = [slice(first, first + PIECE) for first in range(0, series, PIECE)]
    moves = [(sector_hbm, sector_ref), (loadings_hbm, loadings_ref)]
    for piece in pieces:
        moves.append((variances_hbm.at[:, piece], variances_ref.at[:, piece]))
        moves.append((returns_hbm.at[:, piece], returns_ref.at[:, piece]))
    row = lax.axis_index("rows")
    columns = pl.ds(pl.multiple_of(row // 2 * LANES, LANES), LANES)
    moves.append((noise_hbm.at[:, columns], noise_ref))
    moves.append((decay_hbm.at[:, columns], decay_ref))
    copies = [pltpu.make_async_copy(*move, sems.at[index]) for index, move in enumerate(moves)]
    for copy in copies:
        copy.start()
    copies[0].wait()
    owner = lax.broadcasted_iota(jnp.int32, (factors, PIECE), 0)
    one_hot = [
        jnp.where(owner == sector_ref[:, piece], 1.0, 0.0).astype(jnp.bfloat16) for piece in pieces
    ]
    copies[1].wait()
    both = jnp.zeros((4 * bars, factors), jnp.float32)
    for index, piece in enumerate(pieces):
        copies[2 + 2 * index].wait()
        copies[3 + 2 * index].wait()
        loadings = loadings_ref[:, piece]
        scaled = loadings / variances_ref[:, piece]
        stacked = jnp.concatenate([returns_ref[:, piece] * scaled, scaled * loadings], axis=0)
        upper = stacked.astype(jnp.bfloat16)
        lower = (stacked - upper.astype(jnp.float32)).astype(jnp.bfloat16)
        both += lax.dot_general(
            jnp.concatenate([upper, lower], axis=0),
            one_hot[index],
            (((1,), (1,)), ((), ())),
            preferred_element_type=jnp.float32,
        )
    total = both[: 2 * bars] + both[2 * bars :]
    half = bars // 2
    low_lanes = lax.broadcasted_iota(jnp.int32, (half, LANES), 1) < HALF
    copies[-2].wait()
    copies[-1].wait()
    upper_half = jnp.full((half, LANES), row % 2, jnp.int32) == 1
    early, late = noise_ref[:half, :], noise_ref[half:, :]
    noise_out[...] = jnp.where(
        low_lanes,
        jnp.where(upper_half, pltpu.roll(early, HALF, 1), early),
        jnp.where(upper_half, late, pltpu.roll(late, HALF, 1)),
    )
    decay = decay_ref[...]
    decay_out[...] = jnp.where(low_lanes[:1] == upper_half[:1], pltpu.roll(decay, HALF, 1), decay)
    slots = row_order(peers)
    for pair in range(factors // LANES):
        columns = slice(pair * LANES, (pair + 1) * LANES)
        for kind in range(2):
            first = total[kind * bars : kind * bars + half, columns]
            second = total[kind * bars + half : (kind + 1) * bars, columns]
            rows = slice(kind * half, (kind + 1) * half)
            out_ref[slots.index(2 * pair), rows, :] = jnp.where(low_lanes, first, pltpu.roll(second, HALF, 1))
            out_ref[slots.index(2 * pair + 1), rows, :] = jnp.where(low_lanes, pltpu.roll(first, HALF, 1), second)


def added(terms):
    while len(terms) > 1:
        terms = [sum(terms[i + 1 : i + 2], terms[i]) for i in range(0, len(terms), 2)]
    return terms[0]


def block_kernel(parts_ref, noise_ref, decay_ref, local_ref, summary_hbm, summary_ref, sem):
    peers, rows, _ = parts_ref.shape
    half = rows // 2
    depth = half // SUB
    lane, sub = iotas()
    decay = decay_ref[...]
    elements = []
    for step in range(depth):
        signal = added([parts_ref[peer, pl.ds(step, SUB, stride=depth), :] for peer in range(peers)])
        information = added(
            [parts_ref[peer, pl.ds(half + step, SUB, stride=depth), :] for peer in range(peers)]
        )
        noise = noise_ref[pl.ds(step, SUB, stride=depth), :]
        inverse = 1.0 / (1.0 + noise * information)
        decayed = decay * inverse
        scaled = noise * inverse
        elements.append((decayed, scaled * signal, scaled, decayed * signal, decay * decayed * information))
    forward = [elements[0]]
    for step in range(1, depth):
        forward.append(combine(forward[-1], elements[step]))
    backward = [None] * depth
    running = elements[-1]
    for step in range(depth - 2, -1, -1):
        backward[step] = running
        running = combine(elements[step], running)
    total = forward[-1]
    ahead, behind = total, total
    for shift in (1, 2, 4):
        ahead = combine(keep(sub >= shift, rolled(ahead, shift, 0)), ahead)
        behind = combine(behind, keep(sub < SUB - shift, rolled(behind, SUB - shift, 0)))
    other = tuple(
        jnp.broadcast_to(pltpu.roll(part[SUB - 1 :, :], HALF, 1), (SUB, LANES)) for part in ahead
    )
    before = combine(keep(lane >= HALF, other), keep(sub >= 1, rolled(ahead, 1, 0)))
    after = combine(keep(sub < SUB - 1, rolled(behind, SUB - 1, 0)), keep(lane < HALF, other))
    whole = combine(other, ahead)
    low = lane[:1, :] < HALF
    rows = [part[SUB - 1 :, :] for part in whole]
    turned = [pltpu.roll(row, HALF, 1) for row in rows]
    packed = jnp.concatenate(
        [
            jnp.where(low, turned[0], rows[1]),
            jnp.where(low, turned[2], rows[3]),
            jnp.where(low, turned[4], rows[4]),
            jnp.zeros((1, LANES), jnp.float32),
        ],
        axis=0,
    )
    for peer in range(summary_ref.shape[0]):
        summary_ref[peer] = packed
    copy = pltpu.make_async_copy(summary_ref, summary_hbm, sem)
    copy.start()
    slot = 0
    for element in (before, after, *forward, *backward[:-1]):
        for part in element:
            local_ref[slot] = part
            slot += 1
    copy.wait()


def swapped(element, low):
    mask = lax.broadcasted_iota(jnp.int32, (1, LANES), 1) < HALF
    turn = rolled(element, HALF, 1)
    return tuple(
        jnp.where(mask, own, other) if low else jnp.where(mask, other, own) for own, other in zip(element, turn)
    )


def product(element):
    for shift in (1, 2, 4):
        element = combine(element, rolled(element, SUB - shift, 0))
    return tuple(part[:1, :] for part in element)


def finish_kernel(local_ref, received_ref, mean_ref, log_ref, sorted_ref):
    depth = (local_ref.shape[0] // 5 - 1) // 2
    place = lax.axis_index("tm")
    lane, sub = iotas()
    low = lane < HALF
    strip = received_ref.shape[0] // SUB
    for slot, block in enumerate(block_order(received_ref.shape[0])):
        sorted_ref[4 * block : 4 * block + 4, :] = received_ref[slot]
    pieces = []
    for step in range(strip):
        raw = [sorted_ref[pl.ds(4 * step + kind, SUB, stride=4 * strip), :] for kind in range(3)]
        turn = [pltpu.roll(part, HALF, 1) for part in raw[:2]]
        element = (
            jnp.where(low, raw[0], turn[0]),
            jnp.where(low, turn[0], raw[0]),
            jnp.where(low, raw[1], turn[1]),
            jnp.where(low, turn[1], raw[1]),
            raw[2],
        )
        block = sub * strip + step
        pieces.append(keep(jnp.where(low, block - place, place - block) < 0, element))
    while len(pieces) > 1:
        pieces = [combine(pieces[i], pieces[i + 1]) for i in range(0, len(pieces), 2)]
    total = product(pieces[0])
    before, after = swapped(total, True), swapped(total, False)
    mean_in, cov_in = before[1], before[2]
    info_in, prec_in = after[3], after[4]

    def element_at(index):
        return tuple(local_ref[5 * index + part] for part in range(5))

    def push(mean, cov, element):
        gain, shift_mean, shift_cov, info, prec = element
        scaled = gain / (1.0 + cov * prec)
        return scaled * (mean + cov * info) + shift_mean, scaled * gain * cov + shift_cov

    def pull(info, prec, element):
        gain, shift_mean, shift_cov, own_info, own_prec = element
        scaled = gain / (1.0 + shift_cov * prec)
        return scaled * (info - prec * shift_mean) + own_info, scaled * gain * prec + own_prec

    mean_in, cov_in = push(mean_in, cov_in, element_at(0))
    info_in, prec_in = pull(info_in, prec_in, element_at(1))
    for step in range(depth):
        mean, cov = push(mean_in, cov_in, element_at(2 + step))
        if step < depth - 1:
            info, prec = pull(info_in, prec_in, element_at(2 + depth + step))
        else:
            info, prec = info_in, prec_in
        inverse = 1.0 / (1.0 + cov * prec)
        smoothed = (mean + cov * info) * inverse
        logged = jnp.log(cov * inverse)
        for ref, value in ((mean_ref, smoothed), (log_ref, logged)):
            ref[pl.ds(step, SUB, stride=depth), :] = value[:, :HALF]
            ref[pl.ds(SUB * depth + step, SUB, stride=depth), :] = pltpu.roll(value, HALF, 1)[:, :HALF]


VMEM = pl.BlockSpec(memory_space=pltpu.VMEM)


SMALL = pltpu.CompilerParams(vmem_limit_bytes=4 * 1024 * 1024)


def exchanged(x, axis, order):
    return lax.all_to_all(x, axis, 0, 0, axis_index_groups=[order])


def body(returns, variances, loadings, sector, persistence, factor_noise):
    bars, series = returns.shape
    peers = lax.axis_size("rows")
    blocks = lax.axis_size("tm")
    half = bars // 2
    depth = half // SUB
    count = 2 * depth + 1
    inputs = [
        pltpu.with_memory_space_constraint(array, pltpu.HBM)
        for array in (
            returns, variances, loadings[None, :], sector[None, :], factor_noise, persistence[None, :]
        )
    ]
    sends, noise, decay = pl.pallas_call(
        project_kernel,
        out_shape=(
            pltpu.VMEM((peers, bars, LANES), jnp.float32),
            pltpu.VMEM((half, LANES), jnp.float32),
            pltpu.VMEM((1, LANES), jnp.float32),
        ),
        in_specs=[pl.BlockSpec(memory_space=pltpu.HBM)] * 6,
        out_specs=(VMEM, VMEM, VMEM),
        scratch_shapes=[
            pltpu.VMEM((bars, series), jnp.float32),
            pltpu.VMEM((bars, series), jnp.float32),
            pltpu.VMEM((1, series), jnp.float32),
            pltpu.VMEM((1, series), jnp.int32),
            pltpu.VMEM((bars, LANES), jnp.float32),
            pltpu.VMEM((1, LANES), jnp.float32),
            pltpu.SemaphoreType.DMA((4 + 2 * (series // PIECE),)),
        ],
        compiler_params=pltpu.CompilerParams(vmem_limit_bytes=24 * 1024 * 1024),
    )(*inputs)
    parts = exchanged(sends, "rows", row_order(peers))
    local, summary = pl.pallas_call(
        block_kernel,
        out_shape=(
            jax.ShapeDtypeStruct((5 * count, SUB, LANES), jnp.float32),
            jax.ShapeDtypeStruct((blocks, 4, LANES), jnp.float32),
        ),
        in_specs=[VMEM] * 3,
        out_specs=(VMEM, pl.BlockSpec(memory_space=pltpu.HBM)),
        scratch_shapes=[pltpu.VMEM((blocks, 4, LANES), jnp.float32), pltpu.SemaphoreType.DMA],
        compiler_params=SMALL,
    )(parts, noise, decay)
    received = exchanged(summary, "tm", block_order(blocks))
    return pl.pallas_call(
        finish_kernel,
        out_shape=(
            jax.ShapeDtypeStruct((bars, HALF), jnp.float32),
            jax.ShapeDtypeStruct((bars, HALF), jnp.float32),
        ),
        in_specs=[VMEM] * 2,
        out_specs=(VMEM, VMEM),
        scratch_shapes=[pltpu.VMEM((blocks * 4, LANES), jnp.float32)],
        compiler_params=SMALL,
    )(local, received)


def solution(mesh):
    in_specs = (P("tm", "rows"), P("tm", "rows"), P("rows"), P("rows"), P(), P("tm", None))
    out_specs = (P("tm", "rows"), P("tm", "rows"))
    return jax.shard_map(body, mesh=mesh, in_specs=in_specs, out_specs=out_specs, check_vma=False)
```

```python
import functools

import functools

import jax
import jax.numpy as jnp
from jax import lax
from jax.experimental import pallas as pl
from jax.experimental.pallas import tpu as pltpu
from jax.sharding import PartitionSpec as P

SUB = 8
LANES = 128
HALF = 64
PIECE = 1024
NEAR = 16


def row_order(peers):
    first = peers // 2
    return sorted(range(peers), key=lambda y: (y != first, -min((y - first) % peers, (first - y) % peers), y))


def near_order(blocks):
    first = blocks - 2
    length = max(blocks // 2, 1)

    def far(block):
        steps = abs(block // 2 - first // 2)
        return min(steps, length - steps) + block % 2

    return sorted(range(blocks), key=lambda block: (block != first, -far(block), block))


def far_order(blocks):
    first = blocks // 2
    return [(first + i) % blocks for i in range(blocks)]


def combine(earlier, later):
    left_gain, left_mean, left_cov, left_info, left_prec = earlier
    right_gain, right_mean, right_cov, right_info, right_prec = later
    inverse = 1.0 / (1.0 + left_cov * right_prec)
    right_scaled = right_gain * inverse
    left_scaled = left_gain * inverse
    return (
        right_scaled * left_gain,
        right_scaled * (left_mean + left_cov * right_info) + right_mean,
        right_scaled * right_gain * left_cov + right_cov,
        left_scaled * (right_info - right_prec * left_mean) + left_info,
        left_scaled * left_gain * right_prec + left_prec,
    )


def keep(mask, element):
    return tuple(jnp.where(mask, part, fill) for part, fill in zip(element, (1.0, 0.0, 0.0, 0.0, 0.0)))


def rolled(element, shift, axis):
    return tuple(pltpu.roll(part, shift, axis) for part in element)


def iotas():
    lane = lax.broadcasted_iota(jnp.int32, (SUB, LANES), 1)
    sub = lax.broadcasted_iota(jnp.int32, (SUB, LANES), 0)
    return lane, sub


def project_kernel(
    returns_hbm, variances_hbm, loadings_hbm, sector_hbm, noise_hbm, decay_hbm,
    out_ref, noise_out, decay_out,
    returns_ref, variances_ref, loadings_ref, sector_ref, noise_ref, decay_ref, sems,
):
    bars, series = returns_ref.shape
    peers = out_ref.shape[0]
    factors = peers * HALF
    pieces = [slice(first, first + PIECE) for first in range(0, series, PIECE)]
    moves = [(sector_hbm, sector_ref), (loadings_hbm, loadings_ref)]
    for piece in pieces:
        moves.append((variances_hbm.at[:, piece], variances_ref.at[:, piece]))
        moves.append((returns_hbm.at[:, piece], returns_ref.at[:, piece]))
    row = lax.axis_index("rows")
    columns = pl.ds(pl.multiple_of(row // 2 * LANES, LANES), LANES)
    moves.append((noise_hbm.at[:, columns], noise_ref))
    moves.append((decay_hbm.at[:, columns], decay_ref))
    copies = [pltpu.make_async_copy(*move, sems.at[index]) for index, move in enumerate(moves)]
    for copy in copies:
        copy.start()
    copies[0].wait()
    owner = lax.broadcasted_iota(jnp.int32, (factors, PIECE), 0)
    one_hot = [
        jnp.where(owner == sector_ref[:, piece], 1.0, 0.0).astype(jnp.bfloat16) for piece in pieces
    ]
    copies[1].wait()
    both = jnp.zeros((4 * bars, factors), jnp.float32)
    for index, piece in enumerate(pieces):
        copies[2 + 2 * index].wait()
        copies[3 + 2 * index].wait()
        loadings = loadings_ref[:, piece]
        scaled = loadings / variances_ref[:, piece]
        stacked = jnp.concatenate([returns_ref[:, piece] * scaled, scaled * loadings], axis=0)
        upper = stacked.astype(jnp.bfloat16)
        lower = (stacked - upper.astype(jnp.float32)).astype(jnp.bfloat16)
        both += lax.dot_general(
            jnp.concatenate([upper, lower], axis=0),
            one_hot[index],
            (((1,), (1,)), ((), ())),
            preferred_element_type=jnp.float32,
        )
    total = both[: 2 * bars] + both[2 * bars :]
    half = bars // 2
    low_lanes = lax.broadcasted_iota(jnp.int32, (half, LANES), 1) < HALF
    copies[-2].wait()
    copies[-1].wait()
    upper_half = jnp.full((half, LANES), row % 2, jnp.int32) == 1
    early, late = noise_ref[:half, :], noise_ref[half:, :]
    noise_out[...] = jnp.where(
        low_lanes,
        jnp.where(upper_half, pltpu.roll(early, HALF, 1), early),
        jnp.where(upper_half, late, pltpu.roll(late, HALF, 1)),
    )
    decay = decay_ref[...]
    decay_out[...] = jnp.where(low_lanes[:1] == upper_half[:1], pltpu.roll(decay, HALF, 1), decay)
    slots = row_order(peers)
    for pair in range(factors // LANES):
        columns = slice(pair * LANES, (pair + 1) * LANES)
        for kind in range(2):
            first = total[kind * bars : kind * bars + half, columns]
            second = total[kind * bars + half : (kind + 1) * bars, columns]
            rows = slice(kind * half, (kind + 1) * half)
            out_ref[slots.index(2 * pair), rows, :] = jnp.where(low_lanes, first, pltpu.roll(second, HALF, 1))
            out_ref[slots.index(2 * pair + 1), rows, :] = jnp.where(low_lanes, pltpu.roll(first, HALF, 1), second)


def added(terms):
    while len(terms) > 1:
        terms = [sum(terms[i + 1 : i + 2], terms[i]) for i in range(0, len(terms), 2)]
    return terms[0]


def spread(ref, rows):
    tile = jnp.concatenate([*rows, jnp.zeros((SUB - 5, LANES), jnp.float32)], axis=0)
    for peer in range(ref.shape[0]):
        ref[peer] = tile


def block_kernel(parts_ref, noise_ref, decay_ref, local_ref, summary_ref):
    peers, rows, _ = parts_ref.shape
    half = rows // 2
    depth = half // SUB
    lane, sub = iotas()
    decay = decay_ref[...]
    elements = []
    for step in range(depth):
        signal = added([parts_ref[peer, pl.ds(step, SUB, stride=depth), :] for peer in range(peers)])
        information = added(
            [parts_ref[peer, pl.ds(half + step, SUB, stride=depth), :] for peer in range(peers)]
        )
        noise = noise_ref[pl.ds(step, SUB, stride=depth), :]
        inverse = 1.0 / (1.0 + noise * information)
        decayed = decay * inverse
        scaled = noise * inverse
        elements.append((decayed, scaled * signal, scaled, decayed * signal, decay * decayed * information))
    forward = [elements[0]]
    for step in range(1, depth):
        forward.append(combine(forward[-1], elements[step]))
    backward = [None] * depth
    running = elements[-1]
    for step in range(depth - 2, -1, -1):
        backward[step] = running
        running = combine(elements[step], running)
    total = forward[-1]
    ahead, behind = total, total
    for shift in (1, 2, 4):
        ahead = combine(keep(sub >= shift, rolled(ahead, shift, 0)), ahead)
        behind = combine(behind, keep(sub < SUB - shift, rolled(behind, SUB - shift, 0)))
    other = tuple(
        jnp.broadcast_to(pltpu.roll(part[SUB - 1 :, :], HALF, 1), (SUB, LANES)) for part in ahead
    )
    before = combine(keep(lane >= HALF, other), keep(sub >= 1, rolled(ahead, 1, 0)))
    after = combine(keep(sub < SUB - 1, rolled(behind, SUB - 1, 0)), keep(lane < HALF, other))
    whole = combine(other, ahead)
    high = lane[:1, :] >= HALF
    rows = [part[SUB - 1 :, :] for part in whole]
    spread(summary_ref, [jnp.where(high, row, pltpu.roll(row, HALF, 1)) for row in rows])
    slot = 0
    for element in (before, after, *forward, *backward[:-1]):
        for part in element:
            local_ref[slot] = part
            slot += 1


def read_rows(ref):
    return tuple(ref[part : part + 1, :] for part in range(5))


def swapped(element, low):
    mask = lax.broadcasted_iota(jnp.int32, (1, LANES), 1) < HALF
    turn = rolled(element, HALF, 1)
    return tuple(
        jnp.where(mask, own, other) if low else jnp.where(mask, other, own) for own, other in zip(element, turn)
    )


def product(pieces):
    while len(pieces) > 1:
        pieces = [combine(pieces[i], pieces[i + 1]) for i in range(0, len(pieces), 2)]
    total = pieces[0]
    for shift in (1, 2, 4):
        total = combine(total, rolled(total, SUB - shift, 0))
    return tuple(part[:1, :] for part in total)


def members(received_ref, sorted_ref, order):
    for slot, member in enumerate(order):
        sorted_ref[SUB * member : SUB * (member + 1), :] = received_ref[slot]
    strip = sorted_ref.shape[0] // (SUB * SUB)
    sub = lax.broadcasted_iota(jnp.int32, (SUB, LANES), 0)
    pieces = []
    for step in range(strip):
        element = tuple(
            sorted_ref[pl.ds(SUB * step + part, SUB, stride=SUB * strip), :] for part in range(5)
        )
        pieces.append((sub * strip + step, element))
    return pieces


def around(pieces, place, count):
    low = lax.broadcasted_iota(jnp.int32, (SUB, LANES), 1) < HALF
    wanted = []
    for number, element in pieces:
        outside = jnp.where(low, number - place, place - number) < 0
        wanted.append(keep(outside & (number < count), element))
    return product(wanted)


def extended(inner, outer):
    mask = lax.broadcasted_iota(jnp.int32, (1, LANES), 1) < HALF
    earlier = tuple(jnp.where(mask, o, i) for i, o in zip(inner, outer))
    later = tuple(jnp.where(mask, i, o) for i, o in zip(inner, outer))
    return combine(earlier, later)


def level_kernel(received_ref, context_ref, total_ref, sorted_ref):
    count = received_ref.shape[0]
    place = lax.rem(lax.axis_index("tm"), count)
    pieces = members(received_ref, sorted_ref, near_order(count))
    spread(total_ref, product([keep(number < count, element) for number, element in pieces]))
    for part, row in enumerate(around(pieces, place, count)):
        context_ref[part : part + 1, :] = row
    context_ref[5:, :] = jnp.zeros((SUB - 5, LANES), jnp.float32)


def finish_kernel(near, local_ref, context_ref, received_ref, mean_ref, log_ref, sorted_ref):
    depth = (local_ref.shape[0] // 5 - 1) // 2
    count = received_ref.shape[0]
    place = lax.div(lax.axis_index("tm"), near)
    pieces = members(received_ref, sorted_ref, far_order(count))
    total = extended(read_rows(context_ref), around(pieces, place, count))
    before, after = swapped(total, True), swapped(total, False)
    mean_in, cov_in = before[1], before[2]
    info_in, prec_in = after[3], after[4]

    def element_at(index):
        return tuple(local_ref[5 * index + part] for part in range(5))

    def push(mean, cov, element):
        gain, shift_mean, shift_cov, info, prec = element
        scaled = gain / (1.0 + cov * prec)
        return scaled * (mean + cov * info) + shift_mean, scaled * gain * cov + shift_cov

    def pull(info, prec, element):
        gain, shift_mean, shift_cov, own_info, own_prec = element
        scaled = gain / (1.0 + shift_cov * prec)
        return scaled * (info - prec * shift_mean) + own_info, scaled * gain * prec + own_prec

    mean_in, cov_in = push(mean_in, cov_in, element_at(0))
    info_in, prec_in = pull(info_in, prec_in, element_at(1))
    for step in range(depth):
        mean, cov = push(mean_in, cov_in, element_at(2 + step))
        if step < depth - 1:
            info, prec = pull(info_in, prec_in, element_at(2 + depth + step))
        else:
            info, prec = info_in, prec_in
        inverse = 1.0 / (1.0 + cov * prec)
        smoothed = (mean + cov * info) * inverse
        logged = jnp.log(cov * inverse)
        for ref, value in ((mean_ref, smoothed), (log_ref, logged)):
            ref[pl.ds(step, SUB, stride=depth), :] = value[:, :HALF]
            ref[pl.ds(SUB * depth + step, SUB, stride=depth), :] = pltpu.roll(value, HALF, 1)[:, :HALF]


VMEM = pl.BlockSpec(memory_space=pltpu.VMEM)


SMALL = pltpu.CompilerParams(vmem_limit_bytes=4 * 1024 * 1024)


def exchanged(x, axis, groups):
    return lax.all_to_all(x, axis, 0, 0, axis_index_groups=groups)


def sort_scratch(count):
    return pltpu.VMEM((SUB * max(count, SUB), LANES), jnp.float32)


def body(returns, variances, loadings, sector, persistence, factor_noise):
    bars, series = returns.shape
    peers = lax.axis_size("rows")
    blocks = lax.axis_size("tm")
    half = bars // 2
    depth = half // SUB
    count = 2 * depth + 1
    inputs = [
        pltpu.with_memory_space_constraint(array, pltpu.HBM)
        for array in (
            returns, variances, loadings[None, :], sector[None, :], factor_noise, persistence[None, :]
        )
    ]
    sends, noise, decay = pl.pallas_call(
        project_kernel,
        out_shape=(
            pltpu.VMEM((peers, bars, LANES), jnp.float32),
            pltpu.VMEM((half, LANES), jnp.float32),
            pltpu.VMEM((1, LANES), jnp.float32),
        ),
        in_specs=[pl.BlockSpec(memory_space=pltpu.HBM)] * 6,
        out_specs=(VMEM, VMEM, VMEM),
        scratch_shapes=[
            pltpu.VMEM((bars, series), jnp.float32),
            pltpu.VMEM((bars, series), jnp.float32),
            pltpu.VMEM((1, series), jnp.float32),
            pltpu.VMEM((1, series), jnp.int32),
            pltpu.VMEM((bars, LANES), jnp.float32),
            pltpu.VMEM((1, LANES), jnp.float32),
            pltpu.SemaphoreType.DMA((4 + 2 * (series // PIECE),)),
        ],
        compiler_params=pltpu.CompilerParams(vmem_limit_bytes=24 * 1024 * 1024),
    )(*inputs)
    parts = exchanged(sends, "rows", [row_order(peers)])
    near = min(blocks, NEAR)
    far = blocks // near
    local, summary = pl.pallas_call(
        block_kernel,
        out_shape=(
            jax.ShapeDtypeStruct((5 * count, SUB, LANES), jnp.float32),
            jax.ShapeDtypeStruct((near, SUB, LANES), jnp.float32),
        ),
        in_specs=[VMEM] * 3,
        out_specs=(VMEM, VMEM),
        compiler_params=SMALL,
    )(parts, noise, decay)
    groups = [[first + member for member in near_order(near)] for first in range(0, blocks, near)]
    received = exchanged(summary, "tm", groups)
    context, summary = pl.pallas_call(
        level_kernel,
        out_shape=(
            jax.ShapeDtypeStruct((SUB, LANES), jnp.float32),
            jax.ShapeDtypeStruct((far, SUB, LANES), jnp.float32),
        ),
        in_specs=[VMEM],
        out_specs=(VMEM, VMEM),
        scratch_shapes=[sort_scratch(near)],
        compiler_params=SMALL,
    )(received)
    groups = [[first + near * member for member in far_order(far)] for first in range(near)]
    received = exchanged(summary, "tm", groups)
    return pl.pallas_call(
        functools.partial(finish_kernel, near),
        out_shape=(
            jax.ShapeDtypeStruct((bars, HALF), jnp.float32),
            jax.ShapeDtypeStruct((bars, HALF), jnp.float32),
        ),
        in_specs=[VMEM] * 3,
        out_specs=(VMEM, VMEM),
        scratch_shapes=[sort_scratch(far)],
        compiler_params=SMALL,
    )(local, context, received)


def solution(mesh):
    in_specs = (P("tm", "rows"), P("tm", "rows"), P("rows"), P("rows"), P(), P("tm", None))
    out_specs = (P("tm", "rows"), P("tm", "rows"))
    return jax.shard_map(body, mesh=mesh, in_specs=in_specs, out_specs=out_specs, check_vma=False)
```

```python
import functools

import jax
import jax.numpy as jnp
from jax import lax
from jax.experimental import pallas as pl
from jax.experimental.pallas import tpu as pltpu
from jax.sharding import PartitionSpec as P

SUB = 8
LANES = 128
HALF = 64
PIECE = 1024


def row_order(peers):
    first = peers // 2
    return sorted(range(peers), key=lambda y: (y != first, -min((y - first) % peers, (first - y) % peers), y))


def block_order(blocks):
    first = blocks * 23 // 32
    length = max(blocks // 8, 1)

    def start(block):
        return block // 2 % length, -(block % 2), block

    return [first] + [block for block in sorted(range(blocks), key=start) if block != first]


def combine(earlier, later):
    left_gain, left_mean, left_cov, left_info, left_prec = earlier
    right_gain, right_mean, right_cov, right_info, right_prec = later
    inverse = 1.0 / (1.0 + left_cov * right_prec)
    right_scaled = right_gain * inverse
    left_scaled = left_gain * inverse
    return (
        right_scaled * left_gain,
        right_scaled * (left_mean + left_cov * right_info) + right_mean,
        right_scaled * right_gain * left_cov + right_cov,
        left_scaled * (right_info - right_prec * left_mean) + left_info,
        left_scaled * left_gain * right_prec + left_prec,
    )


def keep(mask, element):
    return tuple(jnp.where(mask, part, fill) for part, fill in zip(element, (1.0, 0.0, 0.0, 0.0, 0.0)))


def rolled(element, shift, axis):
    return tuple(pltpu.roll(part, shift, axis) for part in element)


def iotas():
    lane = lax.broadcasted_iota(jnp.int32, (SUB, LANES), 1)
    sub = lax.broadcasted_iota(jnp.int32, (SUB, LANES), 0)
    return lane, sub


def project_kernel(
    returns_hbm, variances_hbm, loadings_hbm, sector_hbm, noise_hbm, decay_hbm,
    out_ref, noise_out, decay_out,
    returns_ref, variances_ref, loadings_ref, sector_ref, noise_ref, decay_ref, sems,
):
    bars, series = returns_ref.shape
    peers = out_ref.shape[0]
    factors = peers * HALF
    pieces = [slice(first, first + PIECE) for first in range(0, series, PIECE)]
    moves = [(sector_hbm, sector_ref), (loadings_hbm, loadings_ref)]
    for piece in pieces:
        moves.append((variances_hbm.at[:, piece], variances_ref.at[:, piece]))
        moves.append((returns_hbm.at[:, piece], returns_ref.at[:, piece]))
    row = lax.axis_index("rows")
    columns = pl.ds(pl.multiple_of(row // 2 * LANES, LANES), LANES)
    moves.append((noise_hbm.at[:, columns], noise_ref))
    moves.append((decay_hbm.at[:, columns], decay_ref))
    copies = [pltpu.make_async_copy(*move, sems.at[index]) for index, move in enumerate(moves)]
    for copy in copies:
        copy.start()
    copies[0].wait()
    owner = lax.broadcasted_iota(jnp.int16, (factors, PIECE), 0)
    ones, zeros = jnp.ones(owner.shape, jnp.bfloat16), jnp.zeros(owner.shape, jnp.bfloat16)
    one_hot = [
        jnp.where(owner == jnp.broadcast_to(sector_ref[:, piece].astype(jnp.int16), owner.shape), ones, zeros)
        for piece in pieces
    ]
    copies[1].wait()
    both = jnp.zeros((4 * bars, factors), jnp.float32)
    for index, piece in enumerate(pieces):
        copies[2 + 2 * index].wait()
        copies[3 + 2 * index].wait()
        loadings = loadings_ref[:, piece]
        scaled = loadings / variances_ref[:, piece]
        stacked = jnp.concatenate([returns_ref[:, piece] * scaled, scaled * loadings], axis=0)
        upper = stacked.astype(jnp.bfloat16)
        lower = (stacked - upper.astype(jnp.float32)).astype(jnp.bfloat16)
        both += lax.dot_general(
            jnp.concatenate([upper, lower], axis=0),
            one_hot[index],
            (((1,), (1,)), ((), ())),
            preferred_element_type=jnp.float32,
        )
    total = both[: 2 * bars] + both[2 * bars :]
    half = bars // 2
    low_lanes = lax.broadcasted_iota(jnp.int32, (half, LANES), 1) < HALF
    copies[-2].wait()
    copies[-1].wait()
    upper_half = jnp.full((half, LANES), row % 2, jnp.int32) == 1
    early, late = noise_ref[:half, :], noise_ref[half:, :]
    noise_out[...] = jnp.where(
        low_lanes,
        jnp.where(upper_half, pltpu.roll(early, HALF, 1), early),
        jnp.where(upper_half, late, pltpu.roll(late, HALF, 1)),
    )
    decay = decay_ref[...]
    decay_out[...] = jnp.where(low_lanes[:1] == upper_half[:1], pltpu.roll(decay, HALF, 1), decay)
    slots = row_order(peers)
    for pair in range(factors // LANES):
        columns = slice(pair * LANES, (pair + 1) * LANES)
        for kind in range(2):
            first = total[kind * bars : kind * bars + half, columns]
            second = total[kind * bars + half : (kind + 1) * bars, columns]
            rows = slice(kind * half, (kind + 1) * half)
            out_ref[slots.index(2 * pair), rows, :] = jnp.where(low_lanes, first, pltpu.roll(second, HALF, 1))
            out_ref[slots.index(2 * pair + 1), rows, :] = jnp.where(low_lanes, pltpu.roll(first, HALF, 1), second)


def added(terms):
    while len(terms) > 1:
        terms = [sum(terms[i + 1 : i + 2], terms[i]) for i in range(0, len(terms), 2)]
    return terms[0]


def block_kernel(parts_ref, noise_ref, decay_ref, local_ref, summary_ref):
    peers, rows, _ = parts_ref.shape
    half = rows // 2
    depth = half // SUB
    lane, sub = iotas()
    decay = decay_ref[...]
    elements = []
    for step in range(depth):
        signal = added([parts_ref[peer, pl.ds(step, SUB, stride=depth), :] for peer in range(peers)])
        information = added(
            [parts_ref[peer, pl.ds(half + step, SUB, stride=depth), :] for peer in range(peers)]
        )
        noise = noise_ref[pl.ds(step, SUB, stride=depth), :]
        inverse = 1.0 / (1.0 + noise * information)
        decayed = decay * inverse
        scaled = noise * inverse
        elements.append((decayed, scaled * signal, scaled, decayed * signal, decay * decayed * information))
    forward = [elements[0]]
    for step in range(1, depth):
        forward.append(combine(forward[-1], elements[step]))
    backward = [None] * depth
    running = elements[-1]
    for step in range(depth - 2, -1, -1):
        backward[step] = running
        running = combine(elements[step], running)
    total = forward[-1]
    ahead, behind = total, total
    for shift in (1, 2, 4):
        ahead = combine(keep(sub >= shift, rolled(ahead, shift, 0)), ahead)
        behind = combine(behind, keep(sub < SUB - shift, rolled(behind, SUB - shift, 0)))
    other = tuple(
        jnp.broadcast_to(pltpu.roll(part[SUB - 1 :, :], HALF, 1), (SUB, LANES)) for part in ahead
    )
    before = combine(keep(lane >= HALF, other), keep(sub >= 1, rolled(ahead, 1, 0)))
    after = combine(keep(sub < SUB - 1, rolled(behind, SUB - 1, 0)), keep(lane < HALF, other))
    whole = combine(other, ahead)
    low = lane[:1, :] < HALF
    rows = [part[SUB - 1 :, :] for part in whole]
    turned = [pltpu.roll(row, HALF, 1) for row in rows]
    packed = jnp.concatenate(
        [
            jnp.where(low, turned[0], rows[1]),
            jnp.where(low, turned[2], rows[3]),
            jnp.where(low, turned[4], rows[4]),
            jnp.zeros((1, LANES), jnp.float32),
        ],
        axis=0,
    )
    for peer in range(summary_ref.shape[0]):
        summary_ref[peer] = packed
    slot = 0
    for element in (before, after, *forward, *backward[:-1]):
        for part in element:
            local_ref[slot] = part
            slot += 1


def swapped(element, low):
    mask = lax.broadcasted_iota(jnp.int32, (1, LANES), 1) < HALF
    turn = rolled(element, HALF, 1)
    return tuple(
        jnp.where(mask, own, other) if low else jnp.where(mask, other, own) for own, other in zip(element, turn)
    )


def product(element):
    for shift in (1, 2, 4):
        element = combine(element, rolled(element, SUB - shift, 0))
    return tuple(part[:1, :] for part in element)


def finish_kernel(local_ref, received_ref, mean_ref, log_ref, sorted_ref):
    depth = (local_ref.shape[0] // 5 - 1) // 2
    place = lax.axis_index("tm")
    lane, sub = iotas()
    low = lane < HALF
    strip = received_ref.shape[0] // SUB
    for slot, block in enumerate(block_order(received_ref.shape[0])):
        sorted_ref[4 * block : 4 * block + 4, :] = received_ref[slot]
    pieces = []
    for step in range(strip):
        raw = [sorted_ref[pl.ds(4 * step + kind, SUB, stride=4 * strip), :] for kind in range(3)]
        turn = [pltpu.roll(part, HALF, 1) for part in raw[:2]]
        element = (
            jnp.where(low, raw[0], turn[0]),
            jnp.where(low, turn[0], raw[0]),
            jnp.where(low, raw[1], turn[1]),
            jnp.where(low, turn[1], raw[1]),
            raw[2],
        )
        block = sub * strip + step
        pieces.append(keep(jnp.where(low, block - place, place - block) < 0, element))
    while len(pieces) > 1:
        pieces = [combine(pieces[i], pieces[i + 1]) for i in range(0, len(pieces), 2)]
    total = product(pieces[0])
    before, after = swapped(total, True), swapped(total, False)
    mean_in, cov_in = before[1], before[2]
    info_in, prec_in = after[3], after[4]

    def element_at(index):
        return tuple(local_ref[5 * index + part] for part in range(5))

    def push(mean, cov, element):
        gain, shift_mean, shift_cov, info, prec = element
        scaled = gain / (1.0 + cov * prec)
        return scaled * (mean + cov * info) + shift_mean, scaled * gain * cov + shift_cov

    def pull(info, prec, element):
        gain, shift_mean, shift_cov, own_info, own_prec = element
        scaled = gain / (1.0 + shift_cov * prec)
        return scaled * (info - prec * shift_mean) + own_info, scaled * gain * prec + own_prec

    mean_in, cov_in = push(mean_in, cov_in, element_at(0))
    info_in, prec_in = pull(info_in, prec_in, element_at(1))
    for step in range(depth):
        mean, cov = push(mean_in, cov_in, element_at(2 + step))
        if step < depth - 1:
            info, prec = pull(info_in, prec_in, element_at(2 + depth + step))
        else:
            info, prec = info_in, prec_in
        inverse = 1.0 / (1.0 + cov * prec)
        smoothed = (mean + cov * info) * inverse
        logged = jnp.log(cov * inverse)
        for ref, value in ((mean_ref, smoothed), (log_ref, logged)):
            ref[pl.ds(step, SUB, stride=depth), :] = value[:, :HALF]
            ref[pl.ds(SUB * depth + step, SUB, stride=depth), :] = pltpu.roll(value, HALF, 1)[:, :HALF]


VMEM = pl.BlockSpec(memory_space=pltpu.VMEM)


SMALL = pltpu.CompilerParams(vmem_limit_bytes=4 * 1024 * 1024)


def exchanged(x, axis, order):
    return lax.all_to_all(x, axis, 0, 0, axis_index_groups=[order])


def body(returns, variances, loadings, sector, persistence, factor_noise):
    bars, series = returns.shape
    peers = lax.axis_size("rows")
    blocks = lax.axis_size("tm")
    half = bars // 2
    depth = half // SUB
    count = 2 * depth + 1
    inputs = [
        pltpu.with_memory_space_constraint(array, pltpu.HBM)
        for array in (
            returns, variances, loadings[None, :], sector[None, :], factor_noise, persistence[None, :]
        )
    ]
    sends, noise, decay = pl.pallas_call(
        project_kernel,
        out_shape=(
            pltpu.VMEM((peers, bars, LANES), jnp.float32),
            pltpu.VMEM((half, LANES), jnp.float32),
            pltpu.VMEM((1, LANES), jnp.float32),
        ),
        in_specs=[pl.BlockSpec(memory_space=pltpu.HBM)] * 6,
        out_specs=(VMEM, VMEM, VMEM),
        scratch_shapes=[
            pltpu.VMEM((bars, series), jnp.float32),
            pltpu.VMEM((bars, series), jnp.float32),
            pltpu.VMEM((1, series), jnp.float32),
            pltpu.VMEM((1, series), jnp.int32),
            pltpu.VMEM((bars, LANES), jnp.float32),
            pltpu.VMEM((1, LANES), jnp.float32),
            pltpu.SemaphoreType.DMA((4 + 2 * (series // PIECE),)),
        ],
        compiler_params=pltpu.CompilerParams(vmem_limit_bytes=24 * 1024 * 1024),
    )(*inputs)
    parts = exchanged(sends, "rows", row_order(peers))
    local, summary = pl.pallas_call(
        block_kernel,
        out_shape=(
            jax.ShapeDtypeStruct((5 * count, SUB, LANES), jnp.float32),
            jax.ShapeDtypeStruct((blocks, 4, LANES), jnp.float32),
        ),
        in_specs=[VMEM] * 3,
        out_specs=(VMEM, VMEM),
        compiler_params=SMALL,
    )(parts, noise, decay)
    received = exchanged(summary, "tm", block_order(blocks))
    return pl.pallas_call(
        finish_kernel,
        out_shape=(
            jax.ShapeDtypeStruct((bars, HALF), jnp.float32),
            jax.ShapeDtypeStruct((bars, HALF), jnp.float32),
        ),
        in_specs=[VMEM] * 2,
        out_specs=(VMEM, VMEM),
        scratch_shapes=[pltpu.VMEM((blocks * 4, LANES), jnp.float32)],
        compiler_params=SMALL,
    )(local, received)


def solution(mesh):
    in_specs = (P("tm", "rows"), P("tm", "rows"), P("rows"), P("rows"), P(), P("tm", None))
    out_specs = (P("tm", "rows"), P("tm", "rows"))
    return jax.shard_map(body, mesh=mesh, in_specs=in_specs, out_specs=out_specs, check_vma=False)
```

```python
import functools

import jax
import jax.numpy as jnp
from jax import lax
from jax.experimental import pallas as pl
from jax.experimental.pallas import tpu as pltpu
from jax.sharding import PartitionSpec as P

SUB = 8
LANES = 128
HALF = 64
PIECE = 2048


def row_order(peers):
    first = peers // 2
    return sorted(range(peers), key=lambda y: (y != first, -min((y - first) % peers, (first - y) % peers), y))


def block_order(blocks):
    first = blocks * 23 // 32
    length = max(blocks // 8, 1)

    def start(block):
        z, x = block // 2 % length, block // 2 // length
        return z, x in (1, 2), x, -(block % 2)

    return [first] + [block for block in sorted(range(blocks), key=start) if block != first]


def combine(earlier, later):
    left_gain, left_mean, left_cov, left_info, left_prec = earlier
    right_gain, right_mean, right_cov, right_info, right_prec = later
    inverse = 1.0 / (1.0 + left_cov * right_prec)
    right_scaled = right_gain * inverse
    left_scaled = left_gain * inverse
    return (
        right_scaled * left_gain,
        right_scaled * (left_mean + left_cov * right_info) + right_mean,
        right_scaled * right_gain * left_cov + right_cov,
        left_scaled * (right_info - right_prec * left_mean) + left_info,
        left_scaled * left_gain * right_prec + left_prec,
    )


def keep(mask, element):
    return tuple(jnp.where(mask, part, fill) for part, fill in zip(element, (1.0, 0.0, 0.0, 0.0, 0.0)))


def rolled(element, shift, axis):
    return tuple(pltpu.roll(part, shift, axis) for part in element)


def iotas():
    lane = lax.broadcasted_iota(jnp.int32, (SUB, LANES), 1)
    sub = lax.broadcasted_iota(jnp.int32, (SUB, LANES), 0)
    return lane, sub


def project_kernel(
    returns_hbm, variances_hbm, loadings_hbm, sector_hbm, noise_hbm, decay_hbm,
    out_ref, noise_out, decay_out,
    returns_ref, variances_ref, loadings_ref, sector_ref, noise_ref, decay_ref, sems,
):
    bars, series = returns_ref.shape
    peers = out_ref.shape[0]
    factors = peers * HALF
    pieces = [slice(first, first + PIECE) for first in range(0, series, PIECE)]
    moves = [(sector_hbm, sector_ref), (loadings_hbm, loadings_ref)]
    for piece in pieces:
        moves.append((variances_hbm.at[:, piece], variances_ref.at[:, piece]))
        moves.append((returns_hbm.at[:, piece], returns_ref.at[:, piece]))
    row = lax.axis_index("rows")
    columns = pl.ds(pl.multiple_of(row // 2 * LANES, LANES), LANES)
    moves.append((noise_hbm.at[:, columns], noise_ref))
    moves.append((decay_hbm.at[:, columns], decay_ref))
    copies = [pltpu.make_async_copy(*move, sems.at[index]) for index, move in enumerate(moves)]
    for copy in copies:
        copy.start()
    copies[0].wait()
    owner = lax.broadcasted_iota(jnp.int16, (factors, PIECE), 0)
    ones, zeros = jnp.ones(owner.shape, jnp.bfloat16), jnp.zeros(owner.shape, jnp.bfloat16)
    one_hot = [
        jnp.where(owner == jnp.broadcast_to(sector_ref[:, piece].astype(jnp.int16), owner.shape), ones, zeros)
        for piece in pieces
    ]
    copies[1].wait()
    both = jnp.zeros((4 * bars, factors), jnp.float32)
    for index, piece in enumerate(pieces):
        copies[2 + 2 * index].wait()
        copies[3 + 2 * index].wait()
        loadings = loadings_ref[:, piece]
        scaled = loadings / variances_ref[:, piece]
        stacked = jnp.concatenate([returns_ref[:, piece] * scaled, scaled * loadings], axis=0)
        upper = stacked.astype(jnp.bfloat16)
        lower = (stacked - upper.astype(jnp.float32)).astype(jnp.bfloat16)
        both += lax.dot_general(
            jnp.concatenate([upper, lower], axis=0),
            one_hot[index],
            (((1,), (1,)), ((), ())),
            preferred_element_type=jnp.float32,
        )
    total = both[: 2 * bars] + both[2 * bars :]
    half = bars // 2
    low_lanes = lax.broadcasted_iota(jnp.int32, (half, LANES), 1) < HALF
    copies[-2].wait()
    copies[-1].wait()
    upper_half = jnp.full((half, LANES), row % 2, jnp.int32) == 1
    early, late = noise_ref[:half, :], noise_ref[half:, :]
    noise_out[...] = jnp.where(
        low_lanes,
        jnp.where(upper_half, pltpu.roll(early, HALF, 1), early),
        jnp.where(upper_half, late, pltpu.roll(late, HALF, 1)),
    )
    decay = decay_ref[...]
    decay_out[...] = jnp.where(low_lanes[:1] == upper_half[:1], pltpu.roll(decay, HALF, 1), decay)
    slots = row_order(peers)
    for pair in range(factors // LANES):
        columns = slice(pair * LANES, (pair + 1) * LANES)
        for kind in range(2):
            first = total[kind * bars : kind * bars + half, columns]
            second = total[kind * bars + half : (kind + 1) * bars, columns]
            rows = slice(kind * half, (kind + 1) * half)
            out_ref[slots.index(2 * pair), rows, :] = jnp.where(low_lanes, first, pltpu.roll(second, HALF, 1))
            out_ref[slots.index(2 * pair + 1), rows, :] = jnp.where(low_lanes, pltpu.roll(first, HALF, 1), second)


def added(terms):
    while len(terms) > 1:
        terms = [sum(terms[i + 1 : i + 2], terms[i]) for i in range(0, len(terms), 2)]
    return terms[0]


def block_kernel(parts_ref, noise_ref, decay_ref, local_ref, summary_ref):
    peers, rows, _ = parts_ref.shape
    half = rows // 2
    depth = half // SUB
    lane, sub = iotas()
    decay = decay_ref[...]
    elements = []
    for step in range(depth):
        signal = added([parts_ref[peer, pl.ds(step, SUB, stride=depth), :] for peer in range(peers)])
        information = added(
            [parts_ref[peer, pl.ds(half + step, SUB, stride=depth), :] for peer in range(peers)]
        )
        noise = noise_ref[pl.ds(step, SUB, stride=depth), :]
        inverse = 1.0 / (1.0 + noise * information)
        decayed = decay * inverse
        scaled = noise * inverse
        elements.append((decayed, scaled * signal, scaled, decayed * signal, decay * decayed * information))
    forward = [elements[0]]
    for step in range(1, depth):
        forward.append(combine(forward[-1], elements[step]))
    backward = [None] * depth
    running = elements[-1]
    for step in range(depth - 2, -1, -1):
        backward[step] = running
        running = combine(elements[step], running)
    total = forward[-1]
    ahead, behind = total, total
    for shift in (1, 2, 4):
        ahead = combine(keep(sub >= shift, rolled(ahead, shift, 0)), ahead)
        behind = combine(behind, keep(sub < SUB - shift, rolled(behind, SUB - shift, 0)))
    other = tuple(
        jnp.broadcast_to(pltpu.roll(part[SUB - 1 :, :], HALF, 1), (SUB, LANES)) for part in ahead
    )
    before = combine(keep(lane >= HALF, other), keep(sub >= 1, rolled(ahead, 1, 0)))
    after = combine(keep(sub < SUB - 1, rolled(behind, SUB - 1, 0)), keep(lane < HALF, other))
    whole = combine(other, ahead)
    low = lane[:1, :] < HALF
    rows = [part[SUB - 1 :, :] for part in whole]
    turned = [pltpu.roll(row, HALF, 1) for row in rows]
    packed = jnp.concatenate(
        [
            jnp.where(low, turned[0], rows[1]),
            jnp.where(low, turned[2], rows[3]),
            jnp.where(low, turned[4], rows[4]),
            jnp.zeros((1, LANES), jnp.float32),
        ],
        axis=0,
    )
    for peer in range(summary_ref.shape[0]):
        summary_ref[peer] = packed
    slot = 0
    for element in (before, after, *forward, *backward[:-1]):
        for part in element:
            local_ref[slot] = part
            slot += 1


def swapped(element, low):
    mask = lax.broadcasted_iota(jnp.int32, (1, LANES), 1) < HALF
    turn = rolled(element, HALF, 1)
    return tuple(
        jnp.where(mask, own, other) if low else jnp.where(mask, other, own) for own, other in zip(element, turn)
    )


def product(element):
    for shift in (1, 2, 4):
        element = combine(element, rolled(element, SUB - shift, 0))
    return tuple(part[:1, :] for part in element)


def finish_kernel(local_ref, received_ref, mean_ref, log_ref, sorted_ref):
    depth = (local_ref.shape[0] // 5 - 1) // 2
    place = lax.axis_index("tm")
    lane, sub = iotas()
    low = lane < HALF
    strip = received_ref.shape[0] // SUB
    for slot, block in enumerate(block_order(received_ref.shape[0])):
        sorted_ref[4 * block : 4 * block + 4, :] = received_ref[slot]
    pieces = []
    for step in range(strip):
        raw = [sorted_ref[pl.ds(4 * step + kind, SUB, stride=4 * strip), :] for kind in range(3)]
        turn = [pltpu.roll(part, HALF, 1) for part in raw[:2]]
        element = (
            jnp.where(low, raw[0], turn[0]),
            jnp.where(low, turn[0], raw[0]),
            jnp.where(low, raw[1], turn[1]),
            jnp.where(low, turn[1], raw[1]),
            raw[2],
        )
        block = sub * strip + step
        pieces.append(keep(jnp.where(low, block - place, place - block) < 0, element))
    while len(pieces) > 1:
        pieces = [combine(pieces[i], pieces[i + 1]) for i in range(0, len(pieces), 2)]
    total = product(pieces[0])
    before, after = swapped(total, True), swapped(total, False)
    mean_in, cov_in = before[1], before[2]
    info_in, prec_in = after[3], after[4]

    def element_at(index):
        return tuple(local_ref[5 * index + part] for part in range(5))

    def push(mean, cov, element):
        gain, shift_mean, shift_cov, info, prec = element
        scaled = gain / (1.0 + cov * prec)
        return scaled * (mean + cov * info) + shift_mean, scaled * gain * cov + shift_cov

    def pull(info, prec, element):
        gain, shift_mean, shift_cov, own_info, own_prec = element
        scaled = gain / (1.0 + shift_cov * prec)
        return scaled * (info - prec * shift_mean) + own_info, scaled * gain * prec + own_prec

    mean_in, cov_in = push(mean_in, cov_in, element_at(0))
    info_in, prec_in = pull(info_in, prec_in, element_at(1))
    for step in range(depth):
        mean, cov = push(mean_in, cov_in, element_at(2 + step))
        if step < depth - 1:
            info, prec = pull(info_in, prec_in, element_at(2 + depth + step))
        else:
            info, prec = info_in, prec_in
        inverse = 1.0 / (1.0 + cov * prec)
        smoothed = (mean + cov * info) * inverse
        logged = jnp.log(cov * inverse)
        for ref, value in ((mean_ref, smoothed), (log_ref, logged)):
            ref[pl.ds(step, SUB, stride=depth), :] = value[:, :HALF]
            ref[pl.ds(SUB * depth + step, SUB, stride=depth), :] = pltpu.roll(value, HALF, 1)[:, :HALF]


VMEM = pl.BlockSpec(memory_space=pltpu.VMEM)


SMALL = pltpu.CompilerParams(vmem_limit_bytes=4 * 1024 * 1024)


def exchanged(x, axis, order):
    return lax.all_to_all(x, axis, 0, 0, axis_index_groups=[order])


def body(returns, variances, loadings, sector, persistence, factor_noise):
    bars, series = returns.shape
    peers = lax.axis_size("rows")
    blocks = lax.axis_size("tm")
    half = bars // 2
    depth = half // SUB
    count = 2 * depth + 1
    inputs = [
        pltpu.with_memory_space_constraint(array, pltpu.HBM)
        for array in (
            returns, variances, loadings[None, :], sector[None, :], factor_noise, persistence[None, :]
        )
    ]
    sends, noise, decay = pl.pallas_call(
        project_kernel,
        out_shape=(
            pltpu.VMEM((peers, bars, LANES), jnp.float32),
            pltpu.VMEM((half, LANES), jnp.float32),
            pltpu.VMEM((1, LANES), jnp.float32),
        ),
        in_specs=[pl.BlockSpec(memory_space=pltpu.HBM)] * 6,
        out_specs=(VMEM, VMEM, VMEM),
        scratch_shapes=[
            pltpu.VMEM((bars, series), jnp.float32),
            pltpu.VMEM((bars, series), jnp.float32),
            pltpu.VMEM((1, series), jnp.float32),
            pltpu.VMEM((1, series), jnp.int32),
            pltpu.VMEM((bars, LANES), jnp.float32),
            pltpu.VMEM((1, LANES), jnp.float32),
            pltpu.SemaphoreType.DMA((4 + 2 * (series // PIECE),)),
        ],
        compiler_params=pltpu.CompilerParams(vmem_limit_bytes=24 * 1024 * 1024),
    )(*inputs)
    parts = exchanged(sends, "rows", row_order(peers))
    local, summary = pl.pallas_call(
        block_kernel,
        out_shape=(
            jax.ShapeDtypeStruct((5 * count, SUB, LANES), jnp.float32),
            jax.ShapeDtypeStruct((blocks, 4, LANES), jnp.float32),
        ),
        in_specs=[VMEM] * 3,
        out_specs=(VMEM, VMEM),
        compiler_params=SMALL,
    )(parts, noise, decay)
    received = exchanged(summary, "tm", block_order(blocks))
    return pl.pallas_call(
        finish_kernel,
        out_shape=(
            jax.ShapeDtypeStruct((bars, HALF), jnp.float32),
            jax.ShapeDtypeStruct((bars, HALF), jnp.float32),
        ),
        in_specs=[VMEM] * 2,
        out_specs=(VMEM, VMEM),
        scratch_shapes=[pltpu.VMEM((blocks * 4, LANES), jnp.float32)],
        compiler_params=SMALL,
    )(local, received)


def solution(mesh):
    in_specs = (P("tm", "rows"), P("tm", "rows"), P("rows"), P("rows"), P(), P("tm", None))
    out_specs = (P("tm", "rows"), P("tm", "rows"))
    return jax.shard_map(body, mesh=mesh, in_specs=in_specs, out_specs=out_specs, check_vma=False)
```

```python
import functools

import jax
import jax.numpy as jnp
from jax import lax
from jax.experimental import pallas as pl
from jax.experimental.pallas import tpu as pltpu
from jax.sharding import PartitionSpec as P

SUB = 8
LANES = 128
HALF = 64
PIECE = 1024


def row_order(peers):
    first = peers // 2
    return sorted(range(peers), key=lambda y: (y != first, -min((y - first) % peers, (first - y) % peers), y))


def chip_order(chips):
    first = chips * 23 // 32
    length = max(chips // 4, 1)
    return [first] + [chip for chip in sorted(range(chips), key=lambda chip: (chip % length, chip)) if chip != first]


def combine(earlier, later):
    left_gain, left_mean, left_cov, left_info, left_prec = earlier
    right_gain, right_mean, right_cov, right_info, right_prec = later
    inverse = 1.0 / (1.0 + left_cov * right_prec)
    right_scaled = right_gain * inverse
    left_scaled = left_gain * inverse
    return (
        right_scaled * left_gain,
        right_scaled * (left_mean + left_cov * right_info) + right_mean,
        right_scaled * right_gain * left_cov + right_cov,
        left_scaled * (right_info - right_prec * left_mean) + left_info,
        left_scaled * left_gain * right_prec + left_prec,
    )


def keep(mask, element):
    return tuple(jnp.where(mask, part, fill) for part, fill in zip(element, (1.0, 0.0, 0.0, 0.0, 0.0)))


def rolled(element, shift, axis):
    return tuple(pltpu.roll(part, shift, axis) for part in element)


def iotas():
    lane = lax.broadcasted_iota(jnp.int32, (SUB, LANES), 1)
    sub = lax.broadcasted_iota(jnp.int32, (SUB, LANES), 0)
    return lane, sub


def project_kernel(
    returns_hbm, variances_hbm, loadings_hbm, sector_hbm, noise_hbm, decay_hbm,
    out_ref, noise_out, decay_out,
    returns_ref, variances_ref, loadings_ref, sector_ref, noise_ref, decay_ref, sems,
):
    bars, series = returns_ref.shape
    peers = out_ref.shape[0]
    factors = peers * HALF
    pieces = [slice(first, first + PIECE) for first in range(0, series, PIECE)]
    moves = [(sector_hbm, sector_ref), (loadings_hbm, loadings_ref)]
    for piece in pieces:
        moves.append((variances_hbm.at[:, piece], variances_ref.at[:, piece]))
        moves.append((returns_hbm.at[:, piece], returns_ref.at[:, piece]))
    row = lax.axis_index("rows")
    columns = pl.ds(pl.multiple_of(row // 2 * LANES, LANES), LANES)
    moves.append((noise_hbm.at[:, columns], noise_ref))
    moves.append((decay_hbm.at[:, columns], decay_ref))
    copies = [pltpu.make_async_copy(*move, sems.at[index]) for index, move in enumerate(moves)]
    for copy in copies:
        copy.start()
    copies[0].wait()
    owner = lax.broadcasted_iota(jnp.int16, (factors, PIECE), 0)
    ones, zeros = jnp.ones(owner.shape, jnp.bfloat16), jnp.zeros(owner.shape, jnp.bfloat16)
    one_hot = [
        jnp.where(owner == jnp.broadcast_to(sector_ref[:, piece].astype(jnp.int16), owner.shape), ones, zeros)
        for piece in pieces
    ]
    copies[1].wait()
    both = jnp.zeros((4 * bars, factors), jnp.float32)
    for index, piece in enumerate(pieces):
        copies[2 + 2 * index].wait()
        copies[3 + 2 * index].wait()
        loadings = loadings_ref[:, piece]
        scaled = loadings / variances_ref[:, piece]
        stacked = jnp.concatenate([returns_ref[:, piece] * scaled, scaled * loadings], axis=0)
        upper = stacked.astype(jnp.bfloat16)
        lower = (stacked - upper.astype(jnp.float32)).astype(jnp.bfloat16)
        both += lax.dot_general(
            jnp.concatenate([upper, lower], axis=0),
            one_hot[index],
            (((1,), (1,)), ((), ())),
            preferred_element_type=jnp.float32,
        )
    total = both[: 2 * bars] + both[2 * bars :]
    half = bars // 2
    low_lanes = lax.broadcasted_iota(jnp.int32, (half, LANES), 1) < HALF
    copies[-2].wait()
    copies[-1].wait()
    upper_half = jnp.full((half, LANES), row % 2, jnp.int32) == 1
    early, late = noise_ref[:half, :], noise_ref[half:, :]
    noise_out[...] = jnp.where(
        low_lanes,
        jnp.where(upper_half, pltpu.roll(early, HALF, 1), early),
        jnp.where(upper_half, late, pltpu.roll(late, HALF, 1)),
    )
    decay = decay_ref[...]
    decay_out[...] = jnp.where(low_lanes[:1] == upper_half[:1], pltpu.roll(decay, HALF, 1), decay)
    slots = row_order(peers)
    for pair in range(factors // LANES):
        columns = slice(pair * LANES, (pair + 1) * LANES)
        for kind in range(2):
            first = total[kind * bars : kind * bars + half, columns]
            second = total[kind * bars + half : (kind + 1) * bars, columns]
            rows = slice(kind * half, (kind + 1) * half)
            out_ref[slots.index(2 * pair), rows, :] = jnp.where(low_lanes, first, pltpu.roll(second, HALF, 1))
            out_ref[slots.index(2 * pair + 1), rows, :] = jnp.where(low_lanes, pltpu.roll(first, HALF, 1), second)


def added(terms):
    while len(terms) > 1:
        terms = [sum(terms[i + 1 : i + 2], terms[i]) for i in range(0, len(terms), 2)]
    return terms[0]


def block_kernel(parts_ref, noise_ref, decay_ref, local_ref, summary_ref):
    peers, rows, _ = parts_ref.shape
    half = rows // 2
    depth = half // SUB
    lane, sub = iotas()
    decay = decay_ref[...]
    elements = []
    for step in range(depth):
        signal = added([parts_ref[peer, pl.ds(step, SUB, stride=depth), :] for peer in range(peers)])
        information = added(
            [parts_ref[peer, pl.ds(half + step, SUB, stride=depth), :] for peer in range(peers)]
        )
        noise = noise_ref[pl.ds(step, SUB, stride=depth), :]
        inverse = 1.0 / (1.0 + noise * information)
        decayed = decay * inverse
        scaled = noise * inverse
        elements.append((decayed, scaled * signal, scaled, decayed * signal, decay * decayed * information))
    forward = [elements[0]]
    for step in range(1, depth):
        forward.append(combine(forward[-1], elements[step]))
    backward = [None] * depth
    running = elements[-1]
    for step in range(depth - 2, -1, -1):
        backward[step] = running
        running = combine(elements[step], running)
    total = forward[-1]
    ahead, behind = total, total
    for shift in (1, 2, 4):
        ahead = combine(keep(sub >= shift, rolled(ahead, shift, 0)), ahead)
        behind = combine(behind, keep(sub < SUB - shift, rolled(behind, SUB - shift, 0)))
    other = tuple(
        jnp.broadcast_to(pltpu.roll(part[SUB - 1 :, :], HALF, 1), (SUB, LANES)) for part in ahead
    )
    before = combine(keep(lane >= HALF, other), keep(sub >= 1, rolled(ahead, 1, 0)))
    after = combine(keep(sub < SUB - 1, rolled(behind, SUB - 1, 0)), keep(lane < HALF, other))
    whole = combine(other, ahead)
    high = lane[:1, :] >= HALF
    for part in range(5):
        row = whole[part][SUB - 1 :, :]
        summary_ref[part : part + 1, :] = jnp.where(high, row, pltpu.roll(row, HALF, 1))
    summary_ref[5:, :] = jnp.zeros((SUB - 5, LANES), jnp.float32)
    slot = 0
    for element in (before, after, *forward, *backward[:-1]):
        for part in element:
            local_ref[slot] = part
            slot += 1


def swapped(element, low):
    mask = lax.broadcasted_iota(jnp.int32, (1, LANES), 1) < HALF
    turn = rolled(element, HALF, 1)
    return tuple(
        jnp.where(mask, own, other) if low else jnp.where(mask, other, own) for own, other in zip(element, turn)
    )


def product(element):
    for shift in (1, 2, 4):
        element = combine(element, rolled(element, SUB - shift, 0))
    return tuple(part[:1, :] for part in element)


def pair_kernel(own_ref, other_ref, context_ref, summary_ref):
    shape = (1, LANES)
    low = lax.broadcasted_iota(jnp.int32, shape, 1) < HALF
    second = jnp.full(shape, lax.rem(lax.axis_index("tm"), 2), jnp.int32) == 1
    own = tuple(own_ref[part : part + 1, :] for part in range(5))
    other = tuple(other_ref[part : part + 1, :] for part in range(5))
    total = combine(
        tuple(jnp.where(second, b, a) for a, b in zip(own, other)),
        tuple(jnp.where(second, a, b) for a, b in zip(own, other)),
    )
    for part, row in enumerate(keep(low == second, other)):
        context_ref[part : part + 1, :] = row
    context_ref[5:, :] = jnp.zeros((SUB - 5, LANES), jnp.float32)
    packed = jnp.concatenate(
        [
            jnp.where(low, total[0], total[1]),
            jnp.where(low, total[2], total[3]),
            total[4],
            jnp.zeros(shape, jnp.float32),
        ],
        axis=0,
    )
    for peer in range(summary_ref.shape[0]):
        summary_ref[peer] = packed


def extended(inner, outer):
    mask = lax.broadcasted_iota(jnp.int32, (1, LANES), 1) < HALF
    earlier = tuple(jnp.where(mask, o, i) for i, o in zip(inner, outer))
    later = tuple(jnp.where(mask, i, o) for i, o in zip(inner, outer))
    return combine(earlier, later)


def finish_kernel(local_ref, context_ref, received_ref, mean_ref, log_ref, sorted_ref):
    depth = (local_ref.shape[0] // 5 - 1) // 2
    place = lax.div(lax.axis_index("tm"), 2)
    lane, sub = iotas()
    low = lane < HALF
    strip = received_ref.shape[0] // SUB
    for slot, block in enumerate(chip_order(received_ref.shape[0])):
        sorted_ref[4 * block : 4 * block + 4, :] = received_ref[slot]
    pieces = []
    for step in range(strip):
        raw = [sorted_ref[pl.ds(4 * step + kind, SUB, stride=4 * strip), :] for kind in range(3)]
        turn = [pltpu.roll(part, HALF, 1) for part in raw[:2]]
        element = (
            jnp.where(low, raw[0], turn[0]),
            jnp.where(low, turn[0], raw[0]),
            jnp.where(low, raw[1], turn[1]),
            jnp.where(low, turn[1], raw[1]),
            raw[2],
        )
        block = sub * strip + step
        pieces.append(keep(jnp.where(low, block - place, place - block) < 0, element))
    while len(pieces) > 1:
        pieces = [combine(pieces[i], pieces[i + 1]) for i in range(0, len(pieces), 2)]
    context = tuple(context_ref[part : part + 1, :] for part in range(5))
    total = extended(context, product(pieces[0]))
    before, after = swapped(total, True), swapped(total, False)
    mean_in, cov_in = before[1], before[2]
    info_in, prec_in = after[3], after[4]

    def element_at(index):
        return tuple(local_ref[5 * index + part] for part in range(5))

    def push(mean, cov, element):
        gain, shift_mean, shift_cov, info, prec = element
        scaled = gain / (1.0 + cov * prec)
        return scaled * (mean + cov * info) + shift_mean, scaled * gain * cov + shift_cov

    def pull(info, prec, element):
        gain, shift_mean, shift_cov, own_info, own_prec = element
        scaled = gain / (1.0 + shift_cov * prec)
        return scaled * (info - prec * shift_mean) + own_info, scaled * gain * prec + own_prec

    mean_in, cov_in = push(mean_in, cov_in, element_at(0))
    info_in, prec_in = pull(info_in, prec_in, element_at(1))
    for step in range(depth):
        mean, cov = push(mean_in, cov_in, element_at(2 + step))
        if step < depth - 1:
            info, prec = pull(info_in, prec_in, element_at(2 + depth + step))
        else:
            info, prec = info_in, prec_in
        inverse = 1.0 / (1.0 + cov * prec)
        smoothed = (mean + cov * info) * inverse
        logged = jnp.log(cov * inverse)
        for ref, value in ((mean_ref, smoothed), (log_ref, logged)):
            ref[pl.ds(step, SUB, stride=depth), :] = value[:, :HALF]
            ref[pl.ds(SUB * depth + step, SUB, stride=depth), :] = pltpu.roll(value, HALF, 1)[:, :HALF]


VMEM = pl.BlockSpec(memory_space=pltpu.VMEM)


SMALL = pltpu.CompilerParams(vmem_limit_bytes=4 * 1024 * 1024)


def exchanged(x, axis, groups):
    return lax.all_to_all(x, axis, 0, 0, axis_index_groups=groups)


def body(returns, variances, loadings, sector, persistence, factor_noise):
    bars, series = returns.shape
    peers = lax.axis_size("rows")
    blocks = lax.axis_size("tm")
    half = bars // 2
    depth = half // SUB
    count = 2 * depth + 1
    tile = jax.ShapeDtypeStruct((SUB, LANES), jnp.float32)
    inputs = [
        pltpu.with_memory_space_constraint(array, pltpu.HBM)
        for array in (
            returns, variances, loadings[None, :], sector[None, :], factor_noise, persistence[None, :]
        )
    ]
    sends, noise, decay = pl.pallas_call(
        project_kernel,
        out_shape=(
            pltpu.VMEM((peers, bars, LANES), jnp.float32),
            pltpu.VMEM((half, LANES), jnp.float32),
            pltpu.VMEM((1, LANES), jnp.float32),
        ),
        in_specs=[pl.BlockSpec(memory_space=pltpu.HBM)] * 6,
        out_specs=(VMEM, VMEM, VMEM),
        scratch_shapes=[
            pltpu.VMEM((bars, series), jnp.float32),
            pltpu.VMEM((bars, series), jnp.float32),
            pltpu.VMEM((1, series), jnp.float32),
            pltpu.VMEM((1, series), jnp.int32),
            pltpu.VMEM((bars, LANES), jnp.float32),
            pltpu.VMEM((1, LANES), jnp.float32),
            pltpu.SemaphoreType.DMA((4 + 2 * (series // PIECE),)),
        ],
        compiler_params=pltpu.CompilerParams(vmem_limit_bytes=24 * 1024 * 1024),
    )(*inputs)
    parts = exchanged(sends, "rows", [row_order(peers)])
    local, summary = pl.pallas_call(
        block_kernel,
        out_shape=(
            jax.ShapeDtypeStruct((5 * count, SUB, LANES), jnp.float32),
            tile,
        ),
        in_specs=[VMEM] * 3,
        out_specs=(VMEM, VMEM),
        compiler_params=SMALL,
    )(parts, noise, decay)
    other = lax.ppermute(summary, "tm", [(block, block ^ 1) for block in range(blocks)])
    chips = blocks // 2
    context, summary = pl.pallas_call(
        pair_kernel,
        out_shape=(tile, jax.ShapeDtypeStruct((chips, 4, LANES), jnp.float32)),
        in_specs=[VMEM] * 2,
        out_specs=(VMEM, VMEM),
        compiler_params=SMALL,
    )(summary, other)
    received = exchanged(summary, "tm", [[2 * chip + core for chip in chip_order(chips)] for core in range(2)])
    return pl.pallas_call(
        finish_kernel,
        out_shape=(
            jax.ShapeDtypeStruct((bars, HALF), jnp.float32),
            jax.ShapeDtypeStruct((bars, HALF), jnp.float32),
        ),
        in_specs=[VMEM] * 3,
        out_specs=(VMEM, VMEM),
        scratch_shapes=[pltpu.VMEM((chips * 4, LANES), jnp.float32)],
        compiler_params=SMALL,
    )(local, context, received)


def solution(mesh):
    in_specs = (P("tm", "rows"), P("tm", "rows"), P("rows"), P("rows"), P(), P("tm", None))
    out_specs = (P("tm", "rows"), P("tm", "rows"))
    return jax.shard_map(body, mesh=mesh, in_specs=in_specs, out_specs=out_specs, check_vma=False)
```

```python
import functools

import jax
import jax.numpy as jnp
from jax import lax
from jax.experimental import pallas as pl
from jax.experimental.pallas import tpu as pltpu
from jax.sharding import PartitionSpec as P

SUB = 8
LANES = 128
HALF = 64


def row_order(peers):
    first = peers // 2
    return sorted(range(peers), key=lambda y: (y != first, -min((y - first) % peers, (first - y) % peers), y))


def block_order(blocks):
    first = blocks * 23 // 32
    length = max(blocks // 8, 1)

    def start(block):
        return block // 2 % length, -(block % 2), block

    return [first] + [block for block in sorted(range(blocks), key=start) if block != first]


def combine(earlier, later):
    left_gain, left_mean, left_cov, left_info, left_prec = earlier
    right_gain, right_mean, right_cov, right_info, right_prec = later
    inverse = 1.0 / (1.0 + left_cov * right_prec)
    right_scaled = right_gain * inverse
    left_scaled = left_gain * inverse
    return (
        right_scaled * left_gain,
        right_scaled * (left_mean + left_cov * right_info) + right_mean,
        right_scaled * right_gain * left_cov + right_cov,
        left_scaled * (right_info - right_prec * left_mean) + left_info,
        left_scaled * left_gain * right_prec + left_prec,
    )


def keep(mask, element):
    return tuple(jnp.where(mask, part, fill) for part, fill in zip(element, (1.0, 0.0, 0.0, 0.0, 0.0)))


def rolled(element, shift, axis):
    return tuple(pltpu.roll(part, shift, axis) for part in element)


def iotas():
    lane = lax.broadcasted_iota(jnp.int32, (SUB, LANES), 1)
    sub = lax.broadcasted_iota(jnp.int32, (SUB, LANES), 0)
    return lane, sub


def project_kernel(
    returns_hbm, variances_hbm, loadings_hbm, sector_hbm, noise_hbm, decay_hbm,
    out_ref, noise_out, decay_out,
    returns_ref, variances_ref, loadings_ref, sector_ref, noise_ref, decay_ref, sems,
):
    bars, series = returns_ref.shape
    peers = out_ref.shape[0]
    factors = peers * HALF
    half = bars // 2
    moves = [(sector_hbm, sector_ref), (loadings_hbm, loadings_ref)]
    pieces = [slice(0, half), slice(half, bars)]
    for piece in pieces:
        moves.append((variances_hbm.at[piece, :], variances_ref.at[piece, :]))
        moves.append((returns_hbm.at[piece, :], returns_ref.at[piece, :]))
    row = lax.axis_index("rows")
    columns = pl.ds(pl.multiple_of(row // 2 * LANES, LANES), LANES)
    moves.append((noise_hbm.at[:, columns], noise_ref))
    moves.append((decay_hbm.at[:, columns], decay_ref))
    copies = [pltpu.make_async_copy(*move, sems.at[index]) for index, move in enumerate(moves)]
    for copy in copies:
        copy.start()
    copies[0].wait()
    owner = lax.broadcasted_iota(jnp.int16, (factors, series), 0)
    ones, zeros = jnp.ones(owner.shape, jnp.bfloat16), jnp.zeros(owner.shape, jnp.bfloat16)
    one_hot = jnp.where(
        owner == jnp.broadcast_to(sector_ref[...].astype(jnp.int16), owner.shape), ones, zeros
    )
    copies[1].wait()
    loadings = loadings_ref[...]
    totals = []
    for index, piece in enumerate(pieces):
        copies[2 + 2 * index].wait()
        copies[3 + 2 * index].wait()
        scaled = loadings / variances_ref[piece, :]
        stacked = jnp.concatenate([returns_ref[piece, :] * scaled, scaled * loadings], axis=0)
        upper = stacked.astype(jnp.bfloat16)
        lower = (stacked - upper.astype(jnp.float32)).astype(jnp.bfloat16)
        both = lax.dot_general(
            jnp.concatenate([upper, lower], axis=0),
            one_hot,
            (((1,), (1,)), ((), ())),
            preferred_element_type=jnp.float32,
        )
        totals.append(both[:bars] + both[bars:])
    low_lanes = lax.broadcasted_iota(jnp.int32, (half, LANES), 1) < HALF
    copies[-2].wait()
    copies[-1].wait()
    upper_half = jnp.full((half, LANES), row % 2, jnp.int32) == 1
    early, late = noise_ref[:half, :], noise_ref[half:, :]
    noise_out[...] = jnp.where(
        low_lanes,
        jnp.where(upper_half, pltpu.roll(early, HALF, 1), early),
        jnp.where(upper_half, late, pltpu.roll(late, HALF, 1)),
    )
    decay = decay_ref[...]
    decay_out[...] = jnp.where(low_lanes[:1] == upper_half[:1], pltpu.roll(decay, HALF, 1), decay)
    slots = row_order(peers)
    for pair in range(factors // LANES):
        columns = slice(pair * LANES, (pair + 1) * LANES)
        for kind in range(2):
            rows = slice(kind * half, (kind + 1) * half)
            first, second = (total[rows, columns] for total in totals)
            out_ref[slots.index(2 * pair), rows, :] = jnp.where(low_lanes, first, pltpu.roll(second, HALF, 1))
            out_ref[slots.index(2 * pair + 1), rows, :] = jnp.where(low_lanes, pltpu.roll(first, HALF, 1), second)


def added(terms):
    while len(terms) > 1:
        terms = [sum(terms[i + 1 : i + 2], terms[i]) for i in range(0, len(terms), 2)]
    return terms[0]


def block_kernel(parts_ref, noise_ref, decay_ref, local_ref, summary_ref):
    peers, rows, _ = parts_ref.shape
    half = rows // 2
    depth = half // SUB
    lane, sub = iotas()
    decay = decay_ref[...]
    elements = []
    for step in range(depth):
        signal = added([parts_ref[peer, pl.ds(step, SUB, stride=depth), :] for peer in range(peers)])
        information = added(
            [parts_ref[peer, pl.ds(half + step, SUB, stride=depth), :] for peer in range(peers)]
        )
        noise = noise_ref[pl.ds(step, SUB, stride=depth), :]
        inverse = 1.0 / (1.0 + noise * information)
        decayed = decay * inverse
        scaled = noise * inverse
        elements.append((decayed, scaled * signal, scaled, decayed * signal, decay * decayed * information))
    forward = [elements[0]]
    for step in range(1, depth):
        forward.append(combine(forward[-1], elements[step]))
    backward = [None] * depth
    running = elements[-1]
    for step in range(depth - 2, -1, -1):
        backward[step] = running
        running = combine(elements[step], running)
    total = forward[-1]
    ahead, behind = total, total
    for shift in (1, 2, 4):
        ahead = combine(keep(sub >= shift, rolled(ahead, shift, 0)), ahead)
        behind = combine(behind, keep(sub < SUB - shift, rolled(behind, SUB - shift, 0)))
    other = tuple(
        jnp.broadcast_to(pltpu.roll(part[SUB - 1 :, :], HALF, 1), (SUB, LANES)) for part in ahead
    )
    before = combine(keep(lane >= HALF, other), keep(sub >= 1, rolled(ahead, 1, 0)))
    after = combine(keep(sub < SUB - 1, rolled(behind, SUB - 1, 0)), keep(lane < HALF, other))
    whole = combine(other, ahead)
    low = lane[:1, :] < HALF
    rows = [part[SUB - 1 :, :] for part in whole]
    turned = [pltpu.roll(row, HALF, 1) for row in rows]
    packed = jnp.concatenate(
        [
            jnp.where(low, turned[0], rows[1]),
            jnp.where(low, turned[2], rows[3]),
            jnp.where(low, turned[4], rows[4]),
            jnp.zeros((1, LANES), jnp.float32),
        ],
        axis=0,
    )
    for peer in range(summary_ref.shape[0]):
        summary_ref[peer] = packed
    slot = 0
    for element in (before, after, *forward, *backward[:-1]):
        for part in element:
            local_ref[slot] = part
            slot += 1


def swapped(element, low):
    mask = lax.broadcasted_iota(jnp.int32, (1, LANES), 1) < HALF
    turn = rolled(element, HALF, 1)
    return tuple(
        jnp.where(mask, own, other) if low else jnp.where(mask, other, own) for own, other in zip(element, turn)
    )


def product(element):
    for shift in (1, 2, 4):
        element = combine(element, rolled(element, SUB - shift, 0))
    return tuple(part[:1, :] for part in element)


def finish_kernel(local_ref, received_ref, mean_ref, log_ref, sorted_ref):
    depth = (local_ref.shape[0] // 5 - 1) // 2
    place = lax.axis_index("tm")
    lane, sub = iotas()
    low = lane < HALF
    strip = received_ref.shape[0] // SUB
    for slot, block in enumerate(block_order(received_ref.shape[0])):
        sorted_ref[4 * block : 4 * block + 4, :] = received_ref[slot]
    pieces = []
    for step in range(strip):
        raw = [sorted_ref[pl.ds(4 * step + kind, SUB, stride=4 * strip), :] for kind in range(3)]
        turn = [pltpu.roll(part, HALF, 1) for part in raw[:2]]
        element = (
            jnp.where(low, raw[0], turn[0]),
            jnp.where(low, turn[0], raw[0]),
            jnp.where(low, raw[1], turn[1]),
            jnp.where(low, turn[1], raw[1]),
            raw[2],
        )
        block = sub * strip + step
        pieces.append(keep(jnp.where(low, block - place, place - block) < 0, element))
    while len(pieces) > 1:
        pieces = [combine(pieces[i], pieces[i + 1]) for i in range(0, len(pieces), 2)]
    total = product(pieces[0])
    before, after = swapped(total, True), swapped(total, False)
    mean_in, cov_in = before[1], before[2]
    info_in, prec_in = after[3], after[4]

    def element_at(index):
        return tuple(local_ref[5 * index + part] for part in range(5))

    def push(mean, cov, element):
        gain, shift_mean, shift_cov, info, prec = element
        scaled = gain / (1.0 + cov * prec)
        return scaled * (mean + cov * info) + shift_mean, scaled * gain * cov + shift_cov

    def pull(info, prec, element):
        gain, shift_mean, shift_cov, own_info, own_prec = element
        scaled = gain / (1.0 + shift_cov * prec)
        return scaled * (info - prec * shift_mean) + own_info, scaled * gain * prec + own_prec

    mean_in, cov_in = push(mean_in, cov_in, element_at(0))
    info_in, prec_in = pull(info_in, prec_in, element_at(1))
    for step in range(depth):
        mean, cov = push(mean_in, cov_in, element_at(2 + step))
        if step < depth - 1:
            info, prec = pull(info_in, prec_in, element_at(2 + depth + step))
        else:
            info, prec = info_in, prec_in
        inverse = 1.0 / (1.0 + cov * prec)
        smoothed = (mean + cov * info) * inverse
        logged = jnp.log(cov * inverse)
        for ref, value in ((mean_ref, smoothed), (log_ref, logged)):
            ref[pl.ds(step, SUB, stride=depth), :] = value[:, :HALF]
            ref[pl.ds(SUB * depth + step, SUB, stride=depth), :] = pltpu.roll(value, HALF, 1)[:, :HALF]


VMEM = pl.BlockSpec(memory_space=pltpu.VMEM)


SMALL = pltpu.CompilerParams(vmem_limit_bytes=4 * 1024 * 1024)


def exchanged(x, axis, order):
    return lax.all_to_all(x, axis, 0, 0, axis_index_groups=[order])


def body(returns, variances, loadings, sector, persistence, factor_noise):
    bars, series = returns.shape
    peers = lax.axis_size("rows")
    blocks = lax.axis_size("tm")
    half = bars // 2
    depth = half // SUB
    count = 2 * depth + 1
    inputs = [
        pltpu.with_memory_space_constraint(array, pltpu.HBM)
        for array in (
            returns, variances, loadings[None, :], sector[None, :], factor_noise, persistence[None, :]
        )
    ]
    sends, noise, decay = pl.pallas_call(
        project_kernel,
        out_shape=(
            pltpu.VMEM((peers, bars, LANES), jnp.float32),
            pltpu.VMEM((half, LANES), jnp.float32),
            pltpu.VMEM((1, LANES), jnp.float32),
        ),
        in_specs=[pl.BlockSpec(memory_space=pltpu.HBM)] * 6,
        out_specs=(VMEM, VMEM, VMEM),
        scratch_shapes=[
            pltpu.VMEM((bars, series), jnp.float32),
            pltpu.VMEM((bars, series), jnp.float32),
            pltpu.VMEM((1, series), jnp.float32),
            pltpu.VMEM((1, series), jnp.int32),
            pltpu.VMEM((bars, LANES), jnp.float32),
            pltpu.VMEM((1, LANES), jnp.float32),
            pltpu.SemaphoreType.DMA((8,)),
        ],
        compiler_params=pltpu.CompilerParams(vmem_limit_bytes=24 * 1024 * 1024),
    )(*inputs)
    parts = exchanged(sends, "rows", row_order(peers))
    local, summary = pl.pallas_call(
        block_kernel,
        out_shape=(
            jax.ShapeDtypeStruct((5 * count, SUB, LANES), jnp.float32),
            jax.ShapeDtypeStruct((blocks, 4, LANES), jnp.float32),
        ),
        in_specs=[VMEM] * 3,
        out_specs=(VMEM, VMEM),
        compiler_params=SMALL,
    )(parts, noise, decay)
    received = exchanged(summary, "tm", block_order(blocks))
    return pl.pallas_call(
        finish_kernel,
        out_shape=(
            jax.ShapeDtypeStruct((bars, HALF), jnp.float32),
            jax.ShapeDtypeStruct((bars, HALF), jnp.float32),
        ),
        in_specs=[VMEM] * 2,
        out_specs=(VMEM, VMEM),
        scratch_shapes=[pltpu.VMEM((blocks * 4, LANES), jnp.float32)],
        compiler_params=SMALL,
    )(local, received)


def solution(mesh):
    in_specs = (P("tm", "rows"), P("tm", "rows"), P("rows"), P("rows"), P(), P("tm", None))
    out_specs = (P("tm", "rows"), P("tm", "rows"))
    return jax.shard_map(body, mesh=mesh, in_specs=in_specs, out_specs=out_specs, check_vma=False)
```

```python
import functools

import jax
import jax.numpy as jnp
from jax import lax
from jax.experimental import pallas as pl
from jax.experimental.pallas import tpu as pltpu
from jax.sharding import PartitionSpec as P

SUB = 8
LANES = 128
HALF = 64
PIECE = 1024


def row_order(peers):
    first = peers // 2
    return sorted(range(peers), key=lambda y: (y != first, -min((y - first) % peers, (first - y) % peers), y))


def block_order(blocks):
    first = blocks * 23 // 32
    length = max(blocks // 8, 1)

    def start(block):
        return block // 2 % length, -(block % 2), block

    return [first] + [block for block in sorted(range(blocks), key=start) if block != first]


def combine(earlier, later):
    left_gain, left_mean, left_cov, left_info, left_prec = earlier
    right_gain, right_mean, right_cov, right_info, right_prec = later
    inverse = 1.0 / (1.0 + left_cov * right_prec)
    right_scaled = right_gain * inverse
    left_scaled = left_gain * inverse
    return (
        right_scaled * left_gain,
        right_scaled * (left_mean + left_cov * right_info) + right_mean,
        right_scaled * right_gain * left_cov + right_cov,
        left_scaled * (right_info - right_prec * left_mean) + left_info,
        left_scaled * left_gain * right_prec + left_prec,
    )


def keep(mask, element):
    return tuple(jnp.where(mask, part, fill) for part, fill in zip(element, (1.0, 0.0, 0.0, 0.0, 0.0)))


def rolled(element, shift, axis):
    return tuple(pltpu.roll(part, shift, axis) for part in element)


def iotas():
    lane = lax.broadcasted_iota(jnp.int32, (SUB, LANES), 1)
    sub = lax.broadcasted_iota(jnp.int32, (SUB, LANES), 0)
    return lane, sub


def project_kernel(
    returns_hbm, variances_hbm, loadings_hbm, sector_hbm, noise_hbm, decay_hbm,
    out_ref, noise_out, decay_out,
    returns_ref, variances_ref, loadings_ref, sector_ref, noise_ref, decay_ref, sems,
):
    bars, series = returns_ref.shape
    peers = out_ref.shape[0]
    factors = peers * HALF
    pieces = [slice(first, first + PIECE) for first in range(0, series, PIECE)]
    moves = [(sector_hbm, sector_ref), (loadings_hbm, loadings_ref)]
    for piece in pieces:
        moves.append((variances_hbm.at[:, piece], variances_ref.at[:, piece]))
        moves.append((returns_hbm.at[:, piece], returns_ref.at[:, piece]))
    row = lax.axis_index("rows")
    columns = pl.ds(pl.multiple_of(row // 2 * LANES, LANES), LANES)
    moves.append((noise_hbm.at[:, columns], noise_ref))
    moves.append((decay_hbm.at[:, columns], decay_ref))
    copies = [pltpu.make_async_copy(*move, sems.at[index]) for index, move in enumerate(moves)]
    for copy in copies:
        copy.start()
    copies[0].wait()
    owner = lax.broadcasted_iota(jnp.int16, (LANES, factors), 1)
    ones, zeros = jnp.ones(owner.shape, jnp.bfloat16), jnp.zeros(owner.shape, jnp.bfloat16)
    strips = []
    for first in range(0, series, LANES):
        across = jnp.broadcast_to(sector_ref[:, first : first + LANES], (LANES, LANES))
        down = across.T.astype(jnp.int16)
        strips.append(jnp.where(owner == jnp.concatenate([down] * (factors // LANES), axis=1), ones, zeros))
    per_piece = PIECE // LANES
    one_hot = [
        jnp.concatenate(strips[first : first + per_piece], axis=0)
        for first in range(0, len(strips), per_piece)
    ]
    copies[1].wait()
    both = jnp.zeros((4 * bars, factors), jnp.float32)
    for index, piece in enumerate(pieces):
        copies[2 + 2 * index].wait()
        copies[3 + 2 * index].wait()
        loadings = loadings_ref[:, piece]
        scaled = loadings / variances_ref[:, piece]
        stacked = jnp.concatenate([returns_ref[:, piece] * scaled, scaled * loadings], axis=0)
        upper = stacked.astype(jnp.bfloat16)
        lower = (stacked - upper.astype(jnp.float32)).astype(jnp.bfloat16)
        both += lax.dot_general(
            jnp.concatenate([upper, lower], axis=0),
            one_hot[index],
            (((1,), (0,)), ((), ())),
            preferred_element_type=jnp.float32,
        )
    total = both[: 2 * bars] + both[2 * bars :]
    half = bars // 2
    low_lanes = lax.broadcasted_iota(jnp.int32, (half, LANES), 1) < HALF
    copies[-2].wait()
    copies[-1].wait()
    upper_half = jnp.full((half, LANES), row % 2, jnp.int32) == 1
    early, late = noise_ref[:half, :], noise_ref[half:, :]
    noise_out[...] = jnp.where(
        low_lanes,
        jnp.where(upper_half, pltpu.roll(early, HALF, 1), early),
        jnp.where(upper_half, late, pltpu.roll(late, HALF, 1)),
    )
    decay = decay_ref[...]
    decay_out[...] = jnp.where(low_lanes[:1] == upper_half[:1], pltpu.roll(decay, HALF, 1), decay)
    slots = row_order(peers)
    for pair in range(factors // LANES):
        columns = slice(pair * LANES, (pair + 1) * LANES)
        for kind in range(2):
            first = total[kind * bars : kind * bars + half, columns]
            second = total[kind * bars + half : (kind + 1) * bars, columns]
            rows = slice(kind * half, (kind + 1) * half)
            out_ref[slots.index(2 * pair), rows, :] = jnp.where(low_lanes, first, pltpu.roll(second, HALF, 1))
            out_ref[slots.index(2 * pair + 1), rows, :] = jnp.where(low_lanes, pltpu.roll(first, HALF, 1), second)


def added(terms):
    while len(terms) > 1:
        terms = [sum(terms[i + 1 : i + 2], terms[i]) for i in range(0, len(terms), 2)]
    return terms[0]


def block_kernel(parts_ref, noise_ref, decay_ref, local_ref, summary_ref):
    peers, rows, _ = parts_ref.shape
    half = rows // 2
    depth = half // SUB
    lane, sub = iotas()
    decay = decay_ref[...]
    elements = []
    for step in range(depth):
        signal = added([parts_ref[peer, pl.ds(step, SUB, stride=depth), :] for peer in range(peers)])
        information = added(
            [parts_ref[peer, pl.ds(half + step, SUB, stride=depth), :] for peer in range(peers)]
        )
        noise = noise_ref[pl.ds(step, SUB, stride=depth), :]
        inverse = 1.0 / (1.0 + noise * information)
        decayed = decay * inverse
        scaled = noise * inverse
        elements.append((decayed, scaled * signal, scaled, decayed * signal, decay * decayed * information))
    forward = [elements[0]]
    for step in range(1, depth):
        forward.append(combine(forward[-1], elements[step]))
    backward = [None] * depth
    running = elements[-1]
    for step in range(depth - 2, -1, -1):
        backward[step] = running
        running = combine(elements[step], running)
    total = forward[-1]
    ahead, behind = total, total
    for shift in (1, 2, 4):
        ahead = combine(keep(sub >= shift, rolled(ahead, shift, 0)), ahead)
        behind = combine(behind, keep(sub < SUB - shift, rolled(behind, SUB - shift, 0)))
    other = tuple(
        jnp.broadcast_to(pltpu.roll(part[SUB - 1 :, :], HALF, 1), (SUB, LANES)) for part in ahead
    )
    before = combine(keep(lane >= HALF, other), keep(sub >= 1, rolled(ahead, 1, 0)))
    after = combine(keep(sub < SUB - 1, rolled(behind, SUB - 1, 0)), keep(lane < HALF, other))
    whole = combine(other, ahead)
    low = lane[:1, :] < HALF
    rows = [part[SUB - 1 :, :] for part in whole]
    turned = [pltpu.roll(row, HALF, 1) for row in rows]
    packed = jnp.concatenate(
        [
            jnp.where(low, turned[0], rows[1]),
            jnp.where(low, turned[2], rows[3]),
            jnp.where(low, turned[4], rows[4]),
            jnp.zeros((1, LANES), jnp.float32),
        ],
        axis=0,
    )
    for peer in range(summary_ref.shape[0]):
        summary_ref[peer] = packed
    slot = 0
    for element in (before, after, *forward, *backward[:-1]):
        for part in element:
            local_ref[slot] = part
            slot += 1


def swapped(element, low):
    mask = lax.broadcasted_iota(jnp.int32, (1, LANES), 1) < HALF
    turn = rolled(element, HALF, 1)
    return tuple(
        jnp.where(mask, own, other) if low else jnp.where(mask, other, own) for own, other in zip(element, turn)
    )


def product(element):
    for shift in (1, 2, 4):
        element = combine(element, rolled(element, SUB - shift, 0))
    return tuple(part[:1, :] for part in element)


def finish_kernel(local_ref, received_ref, mean_ref, log_ref, sorted_ref):
    depth = (local_ref.shape[0] // 5 - 1) // 2
    place = lax.axis_index("tm")
    lane, sub = iotas()
    low = lane < HALF
    strip = received_ref.shape[0] // SUB
    for slot, block in enumerate(block_order(received_ref.shape[0])):
        sorted_ref[4 * block : 4 * block + 4, :] = received_ref[slot]
    pieces = []
    for step in range(strip):
        raw = [sorted_ref[pl.ds(4 * step + kind, SUB, stride=4 * strip), :] for kind in range(3)]
        turn = [pltpu.roll(part, HALF, 1) for part in raw[:2]]
        element = (
            jnp.where(low, raw[0], turn[0]),
            jnp.where(low, turn[0], raw[0]),
            jnp.where(low, raw[1], turn[1]),
            jnp.where(low, turn[1], raw[1]),
            raw[2],
        )
        block = sub * strip + step
        pieces.append(keep(jnp.where(low, block - place, place - block) < 0, element))
    while len(pieces) > 1:
        pieces = [combine(pieces[i], pieces[i + 1]) for i in range(0, len(pieces), 2)]
    total = product(pieces[0])
    before, after = swapped(total, True), swapped(total, False)
    mean_in, cov_in = before[1], before[2]
    info_in, prec_in = after[3], after[4]

    def element_at(index):
        return tuple(local_ref[5 * index + part] for part in range(5))

    def push(mean, cov, element):
        gain, shift_mean, shift_cov, info, prec = element
        scaled = gain / (1.0 + cov * prec)
        return scaled * (mean + cov * info) + shift_mean, scaled * gain * cov + shift_cov

    def pull(info, prec, element):
        gain, shift_mean, shift_cov, own_info, own_prec = element
        scaled = gain / (1.0 + shift_cov * prec)
        return scaled * (info - prec * shift_mean) + own_info, scaled * gain * prec + own_prec

    mean_in, cov_in = push(mean_in, cov_in, element_at(0))
    info_in, prec_in = pull(info_in, prec_in, element_at(1))
    for step in range(depth):
        mean, cov = push(mean_in, cov_in, element_at(2 + step))
        if step < depth - 1:
            info, prec = pull(info_in, prec_in, element_at(2 + depth + step))
        else:
            info, prec = info_in, prec_in
        inverse = 1.0 / (1.0 + cov * prec)
        smoothed = (mean + cov * info) * inverse
        logged = jnp.log(cov * inverse)
        for ref, value in ((mean_ref, smoothed), (log_ref, logged)):
            ref[pl.ds(step, SUB, stride=depth), :] = value[:, :HALF]
            ref[pl.ds(SUB * depth + step, SUB, stride=depth), :] = pltpu.roll(value, HALF, 1)[:, :HALF]


VMEM = pl.BlockSpec(memory_space=pltpu.VMEM)


SMALL = pltpu.CompilerParams(vmem_limit_bytes=4 * 1024 * 1024)


def exchanged(x, axis, order):
    return lax.all_to_all(x, axis, 0, 0, axis_index_groups=[order])


def body(returns, variances, loadings, sector, persistence, factor_noise):
    bars, series = returns.shape
    peers = lax.axis_size("rows")
    blocks = lax.axis_size("tm")
    half = bars // 2
    depth = half // SUB
    count = 2 * depth + 1
    inputs = [
        pltpu.with_memory_space_constraint(array, pltpu.HBM)
        for array in (
            returns, variances, loadings[None, :], sector[None, :], factor_noise, persistence[None, :]
        )
    ]
    sends, noise, decay = pl.pallas_call(
        project_kernel,
        out_shape=(
            pltpu.VMEM((peers, bars, LANES), jnp.float32),
            pltpu.VMEM((half, LANES), jnp.float32),
            pltpu.VMEM((1, LANES), jnp.float32),
        ),
        in_specs=[pl.BlockSpec(memory_space=pltpu.HBM)] * 6,
        out_specs=(VMEM, VMEM, VMEM),
        scratch_shapes=[
            pltpu.VMEM((bars, series), jnp.float32),
            pltpu.VMEM((bars, series), jnp.float32),
            pltpu.VMEM((1, series), jnp.float32),
            pltpu.VMEM((1, series), jnp.int32),
            pltpu.VMEM((bars, LANES), jnp.float32),
            pltpu.VMEM((1, LANES), jnp.float32),
            pltpu.SemaphoreType.DMA((4 + 2 * (series // PIECE),)),
        ],
        compiler_params=pltpu.CompilerParams(vmem_limit_bytes=24 * 1024 * 1024),
    )(*inputs)
    parts = exchanged(sends, "rows", row_order(peers))
    local, summary = pl.pallas_call(
        block_kernel,
        out_shape=(
            jax.ShapeDtypeStruct((5 * count, SUB, LANES), jnp.float32),
            jax.ShapeDtypeStruct((blocks, 4, LANES), jnp.float32),
        ),
        in_specs=[VMEM] * 3,
        out_specs=(VMEM, VMEM),
        compiler_params=SMALL,
    )(parts, noise, decay)
    received = exchanged(summary, "tm", block_order(blocks))
    return pl.pallas_call(
        finish_kernel,
        out_shape=(
            jax.ShapeDtypeStruct((bars, HALF), jnp.float32),
            jax.ShapeDtypeStruct((bars, HALF), jnp.float32),
        ),
        in_specs=[VMEM] * 2,
        out_specs=(VMEM, VMEM),
        scratch_shapes=[pltpu.VMEM((blocks * 4, LANES), jnp.float32)],
        compiler_params=SMALL,
    )(local, received)


def solution(mesh):
    in_specs = (P("tm", "rows"), P("tm", "rows"), P("rows"), P("rows"), P(), P("tm", None))
    out_specs = (P("tm", "rows"), P("tm", "rows"))
    return jax.shard_map(body, mesh=mesh, in_specs=in_specs, out_specs=out_specs, check_vma=False)
```

```python
import functools

import jax
import jax.numpy as jnp
from jax import lax
from jax.experimental import pallas as pl
from jax.experimental.pallas import tpu as pltpu
from jax.sharding import PartitionSpec as P

SUB = 8
LANES = 128
HALF = 64
PIECE = 1024


def row_order(peers):
    first = peers // 2
    return sorted(range(peers), key=lambda y: (y != first, -min((y - first) % peers, (first - y) % peers), y))


def block_order(blocks):
    first = blocks * 23 // 32
    length = max(blocks // 8, 1)

    def start(block):
        return block // 2 % length, -(block % 2), block

    return [first] + [block for block in sorted(range(blocks), key=start) if block != first]


def combine(earlier, later):
    left_gain, left_mean, left_cov, left_info, left_prec = earlier
    right_gain, right_mean, right_cov, right_info, right_prec = later
    inverse = 1.0 / (1.0 + left_cov * right_prec)
    right_scaled = right_gain * inverse
    left_scaled = left_gain * inverse
    return (
        right_scaled * left_gain,
        right_scaled * (left_mean + left_cov * right_info) + right_mean,
        right_scaled * right_gain * left_cov + right_cov,
        left_scaled * (right_info - right_prec * left_mean) + left_info,
        left_scaled * left_gain * right_prec + left_prec,
    )


def keep(mask, element):
    return tuple(jnp.where(mask, part, fill) for part, fill in zip(element, (1.0, 0.0, 0.0, 0.0, 0.0)))


def rolled(element, shift, axis):
    return tuple(pltpu.roll(part, shift, axis) for part in element)


def iotas():
    lane = lax.broadcasted_iota(jnp.int32, (SUB, LANES), 1)
    sub = lax.broadcasted_iota(jnp.int32, (SUB, LANES), 0)
    return lane, sub


def project_kernel(
    returns_hbm, variances_hbm, loadings_hbm, sector_hbm, noise_hbm, decay_hbm,
    out_ref, noise_out, decay_out,
    returns_ref, variances_ref, loadings_ref, sector_ref, noise_ref, decay_ref, sems,
):
    bars, series = returns_ref.shape
    peers = out_ref.shape[0]
    factors = peers * HALF
    pieces = [slice(first, first + PIECE) for first in range(0, series, PIECE)]
    moves = [(sector_hbm, sector_ref), (loadings_hbm, loadings_ref)]
    for piece in pieces:
        moves.append((variances_hbm.at[:, piece], variances_ref.at[:, piece]))
        moves.append((returns_hbm.at[:, piece], returns_ref.at[:, piece]))
    row = lax.axis_index("rows")
    columns = pl.ds(pl.multiple_of(row // 2 * LANES, LANES), LANES)
    moves.append((noise_hbm.at[:, columns], noise_ref))
    moves.append((decay_hbm.at[:, columns], decay_ref))
    copies = [pltpu.make_async_copy(*move, sems.at[index]) for index, move in enumerate(moves)]
    for copy in copies:
        copy.start()
    copies[0].wait()
    owner = lax.broadcasted_iota(jnp.int16, (factors, PIECE), 0)
    ones, zeros = jnp.ones(owner.shape, jnp.bfloat16), jnp.zeros(owner.shape, jnp.bfloat16)
    one_hot = [
        jnp.where(owner == jnp.broadcast_to(sector_ref[:, piece].astype(jnp.int16), owner.shape), ones, zeros)
        for piece in pieces
    ]
    copies[1].wait()
    both = jnp.zeros((factors, 4 * bars), jnp.float32)
    for index, piece in enumerate(pieces):
        copies[2 + 2 * index].wait()
        copies[3 + 2 * index].wait()
        loadings = loadings_ref[:, piece]
        scaled = loadings / variances_ref[:, piece]
        stacked = jnp.concatenate([returns_ref[:, piece] * scaled, scaled * loadings], axis=0)
        upper = stacked.astype(jnp.bfloat16)
        lower = (stacked - upper.astype(jnp.float32)).astype(jnp.bfloat16)
        both += lax.dot_general(
            one_hot[index],
            jnp.concatenate([upper, lower], axis=0),
            (((1,), (1,)), ((), ())),
            preferred_element_type=jnp.float32,
        )
    across = both[:, : 2 * bars] + both[:, 2 * bars :]
    half = bars // 2
    low_lanes = lax.broadcasted_iota(jnp.int32, (half, LANES), 1) < HALF
    copies[-2].wait()
    copies[-1].wait()
    upper_half = jnp.full((half, LANES), row % 2, jnp.int32) == 1
    early, late = noise_ref[:half, :], noise_ref[half:, :]
    noise_out[...] = jnp.where(
        low_lanes,
        jnp.where(upper_half, pltpu.roll(early, HALF, 1), early),
        jnp.where(upper_half, late, pltpu.roll(late, HALF, 1)),
    )
    decay = decay_ref[...]
    decay_out[...] = jnp.where(low_lanes[:1] == upper_half[:1], pltpu.roll(decay, HALF, 1), decay)
    slots = row_order(peers)
    for pair in range(factors // LANES):
        total = across[pair * LANES : (pair + 1) * LANES].T
        for kind in range(2):
            first = total[kind * bars : kind * bars + half]
            second = total[kind * bars + half : (kind + 1) * bars]
            rows = slice(kind * half, (kind + 1) * half)
            out_ref[slots.index(2 * pair), rows, :] = jnp.where(low_lanes, first, pltpu.roll(second, HALF, 1))
            out_ref[slots.index(2 * pair + 1), rows, :] = jnp.where(low_lanes, pltpu.roll(first, HALF, 1), second)


def added(terms):
    while len(terms) > 1:
        terms = [sum(terms[i + 1 : i + 2], terms[i]) for i in range(0, len(terms), 2)]
    return terms[0]


def block_kernel(parts_ref, noise_ref, decay_ref, local_ref, summary_ref):
    peers, rows, _ = parts_ref.shape
    half = rows // 2
    depth = half // SUB
    lane, sub = iotas()
    decay = decay_ref[...]
    elements = []
    for step in range(depth):
        signal = added([parts_ref[peer, pl.ds(step, SUB, stride=depth), :] for peer in range(peers)])
        information = added(
            [parts_ref[peer, pl.ds(half + step, SUB, stride=depth), :] for peer in range(peers)]
        )
        noise = noise_ref[pl.ds(step, SUB, stride=depth), :]
        inverse = 1.0 / (1.0 + noise * information)
        decayed = decay * inverse
        scaled = noise * inverse
        elements.append((decayed, scaled * signal, scaled, decayed * signal, decay * decayed * information))
    forward = [elements[0]]
    for step in range(1, depth):
        forward.append(combine(forward[-1], elements[step]))
    backward = [None] * depth
    running = elements[-1]
    for step in range(depth - 2, -1, -1):
        backward[step] = running
        running = combine(elements[step], running)
    total = forward[-1]
    ahead, behind = total, total
    for shift in (1, 2, 4):
        ahead = combine(keep(sub >= shift, rolled(ahead, shift, 0)), ahead)
        behind = combine(behind, keep(sub < SUB - shift, rolled(behind, SUB - shift, 0)))
    other = tuple(
        jnp.broadcast_to(pltpu.roll(part[SUB - 1 :, :], HALF, 1), (SUB, LANES)) for part in ahead
    )
    before = combine(keep(lane >= HALF, other), keep(sub >= 1, rolled(ahead, 1, 0)))
    after = combine(keep(sub < SUB - 1, rolled(behind, SUB - 1, 0)), keep(lane < HALF, other))
    whole = combine(other, ahead)
    low = lane[:1, :] < HALF
    rows = [part[SUB - 1 :, :] for part in whole]
    turned = [pltpu.roll(row, HALF, 1) for row in rows]
    packed = jnp.concatenate(
        [
            jnp.where(low, turned[0], rows[1]),
            jnp.where(low, turned[2], rows[3]),
            jnp.where(low, turned[4], rows[4]),
            jnp.zeros((1, LANES), jnp.float32),
        ],
        axis=0,
    )
    for peer in range(summary_ref.shape[0]):
        summary_ref[peer] = packed
    slot = 0
    for element in (before, after, *forward, *backward[:-1]):
        for part in element:
            local_ref[slot] = part
            slot += 1


def swapped(element, low):
    mask = lax.broadcasted_iota(jnp.int32, (1, LANES), 1) < HALF
    turn = rolled(element, HALF, 1)
    return tuple(
        jnp.where(mask, own, other) if low else jnp.where(mask, other, own) for own, other in zip(element, turn)
    )


def product(element):
    for shift in (1, 2, 4):
        element = combine(element, rolled(element, SUB - shift, 0))
    return tuple(part[:1, :] for part in element)


def finish_kernel(local_ref, received_ref, mean_ref, log_ref, sorted_ref):
    depth = (local_ref.shape[0] // 5 - 1) // 2
    place = lax.axis_index("tm")
    lane, sub = iotas()
    low = lane < HALF
    strip = received_ref.shape[0] // SUB
    for slot, block in enumerate(block_order(received_ref.shape[0])):
        sorted_ref[4 * block : 4 * block + 4, :] = received_ref[slot]
    pieces = []
    for step in range(strip):
        raw = [sorted_ref[pl.ds(4 * step + kind, SUB, stride=4 * strip), :] for kind in range(3)]
        turn = [pltpu.roll(part, HALF, 1) for part in raw[:2]]
        element = (
            jnp.where(low, raw[0], turn[0]),
            jnp.where(low, turn[0], raw[0]),
            jnp.where(low, raw[1], turn[1]),
            jnp.where(low, turn[1], raw[1]),
            raw[2],
        )
        block = sub * strip + step
        pieces.append(keep(jnp.where(low, block - place, place - block) < 0, element))
    while len(pieces) > 1:
        pieces = [combine(pieces[i], pieces[i + 1]) for i in range(0, len(pieces), 2)]
    total = product(pieces[0])
    before, after = swapped(total, True), swapped(total, False)
    mean_in, cov_in = before[1], before[2]
    info_in, prec_in = after[3], after[4]

    def element_at(index):
        return tuple(local_ref[5 * index + part] for part in range(5))

    def push(mean, cov, element):
        gain, shift_mean, shift_cov, info, prec = element
        scaled = gain / (1.0 + cov * prec)
        return scaled * (mean + cov * info) + shift_mean, scaled * gain * cov + shift_cov

    def pull(info, prec, element):
        gain, shift_mean, shift_cov, own_info, own_prec = element
        scaled = gain / (1.0 + shift_cov * prec)
        return scaled * (info - prec * shift_mean) + own_info, scaled * gain * prec + own_prec

    mean_in, cov_in = push(mean_in, cov_in, element_at(0))
    info_in, prec_in = pull(info_in, prec_in, element_at(1))
    for step in range(depth):
        mean, cov = push(mean_in, cov_in, element_at(2 + step))
        if step < depth - 1:
            info, prec = pull(info_in, prec_in, element_at(2 + depth + step))
        else:
            info, prec = info_in, prec_in
        inverse = 1.0 / (1.0 + cov * prec)
        smoothed = (mean + cov * info) * inverse
        logged = jnp.log(cov * inverse)
        for ref, value in ((mean_ref, smoothed), (log_ref, logged)):
            ref[pl.ds(step, SUB, stride=depth), :] = value[:, :HALF]
            ref[pl.ds(SUB * depth + step, SUB, stride=depth), :] = pltpu.roll(value, HALF, 1)[:, :HALF]


VMEM = pl.BlockSpec(memory_space=pltpu.VMEM)


SMALL = pltpu.CompilerParams(vmem_limit_bytes=4 * 1024 * 1024)


def exchanged(x, axis, order):
    return lax.all_to_all(x, axis, 0, 0, axis_index_groups=[order])


def body(returns, variances, loadings, sector, persistence, factor_noise):
    bars, series = returns.shape
    peers = lax.axis_size("rows")
    blocks = lax.axis_size("tm")
    half = bars // 2
    depth = half // SUB
    count = 2 * depth + 1
    inputs = [
        pltpu.with_memory_space_constraint(array, pltpu.HBM)
        for array in (
            returns, variances, loadings[None, :], sector[None, :], factor_noise, persistence[None, :]
        )
    ]
    sends, noise, decay = pl.pallas_call(
        project_kernel,
        out_shape=(
            pltpu.VMEM((peers, bars, LANES), jnp.float32),
            pltpu.VMEM((half, LANES), jnp.float32),
            pltpu.VMEM((1, LANES), jnp.float32),
        ),
        in_specs=[pl.BlockSpec(memory_space=pltpu.HBM)] * 6,
        out_specs=(VMEM, VMEM, VMEM),
        scratch_shapes=[
            pltpu.VMEM((bars, series), jnp.float32),
            pltpu.VMEM((bars, series), jnp.float32),
            pltpu.VMEM((1, series), jnp.float32),
            pltpu.VMEM((1, series), jnp.int32),
            pltpu.VMEM((bars, LANES), jnp.float32),
            pltpu.VMEM((1, LANES), jnp.float32),
            pltpu.SemaphoreType.DMA((4 + 2 * (series // PIECE),)),
        ],
        compiler_params=pltpu.CompilerParams(vmem_limit_bytes=24 * 1024 * 1024),
    )(*inputs)
    parts = exchanged(sends, "rows", row_order(peers))
    local, summary = pl.pallas_call(
        block_kernel,
        out_shape=(
            jax.ShapeDtypeStruct((5 * count, SUB, LANES), jnp.float32),
            jax.ShapeDtypeStruct((blocks, 4, LANES), jnp.float32),
        ),
        in_specs=[VMEM] * 3,
        out_specs=(VMEM, VMEM),
        compiler_params=SMALL,
    )(parts, noise, decay)
    received = exchanged(summary, "tm", block_order(blocks))
    return pl.pallas_call(
        finish_kernel,
        out_shape=(
            jax.ShapeDtypeStruct((bars, HALF), jnp.float32),
            jax.ShapeDtypeStruct((bars, HALF), jnp.float32),
        ),
        in_specs=[VMEM] * 2,
        out_specs=(VMEM, VMEM),
        scratch_shapes=[pltpu.VMEM((blocks * 4, LANES), jnp.float32)],
        compiler_params=SMALL,
    )(local, received)


def solution(mesh):
    in_specs = (P("tm", "rows"), P("tm", "rows"), P("rows"), P("rows"), P(), P("tm", None))
    out_specs = (P("tm", "rows"), P("tm", "rows"))
    return jax.shard_map(body, mesh=mesh, in_specs=in_specs, out_specs=out_specs, check_vma=False)
```

```python
import functools

import jax
import jax.numpy as jnp
from jax import lax
from jax.experimental import pallas as pl
from jax.experimental.pallas import tpu as pltpu
from jax.sharding import PartitionSpec as P

SUB = 8
LANES = 128
HALF = 64
PIECE = 1024


def row_order(peers):
    first = peers // 2
    return sorted(range(peers), key=lambda y: (y != first, min((y - first) % peers, (first - y) % peers), y))


def block_order(blocks):
    first = blocks * 23 // 32
    length = max(blocks // 8, 1)

    def start(block):
        return block // 2 % length, -(block % 2), block

    return [first] + [block for block in sorted(range(blocks), key=start) if block != first]


def combine(earlier, later):
    left_gain, left_mean, left_cov, left_info, left_prec = earlier
    right_gain, right_mean, right_cov, right_info, right_prec = later
    inverse = 1.0 / (1.0 + left_cov * right_prec)
    right_scaled = right_gain * inverse
    left_scaled = left_gain * inverse
    return (
        right_scaled * left_gain,
        right_scaled * (left_mean + left_cov * right_info) + right_mean,
        right_scaled * right_gain * left_cov + right_cov,
        left_scaled * (right_info - right_prec * left_mean) + left_info,
        left_scaled * left_gain * right_prec + left_prec,
    )


def keep(mask, element):
    return tuple(jnp.where(mask, part, fill) for part, fill in zip(element, (1.0, 0.0, 0.0, 0.0, 0.0)))


def rolled(element, shift, axis):
    return tuple(pltpu.roll(part, shift, axis) for part in element)


def iotas():
    lane = lax.broadcasted_iota(jnp.int32, (SUB, LANES), 1)
    sub = lax.broadcasted_iota(jnp.int32, (SUB, LANES), 0)
    return lane, sub


def project_kernel(
    returns_hbm, variances_hbm, loadings_hbm, sector_hbm, noise_hbm, decay_hbm,
    out_ref, noise_out, decay_out,
    returns_ref, variances_ref, loadings_ref, sector_ref, noise_ref, decay_ref, sems,
):
    bars, series = returns_ref.shape
    peers = out_ref.shape[0]
    factors = peers * HALF
    pieces = [slice(first, first + PIECE) for first in range(0, series, PIECE)]
    moves = [(sector_hbm, sector_ref), (loadings_hbm, loadings_ref)]
    for piece in pieces:
        moves.append((variances_hbm.at[:, piece], variances_ref.at[:, piece]))
        moves.append((returns_hbm.at[:, piece], returns_ref.at[:, piece]))
    row = lax.axis_index("rows")
    columns = pl.ds(pl.multiple_of(row // 2 * LANES, LANES), LANES)
    moves.append((noise_hbm.at[:, columns], noise_ref))
    moves.append((decay_hbm.at[:, columns], decay_ref))
    copies = [pltpu.make_async_copy(*move, sems.at[index]) for index, move in enumerate(moves)]
    for copy in copies:
        copy.start()
    copies[0].wait()
    owner = lax.broadcasted_iota(jnp.int16, (factors, PIECE), 0)
    ones, zeros = jnp.ones(owner.shape, jnp.bfloat16), jnp.zeros(owner.shape, jnp.bfloat16)
    one_hot = [
        jnp.where(owner == jnp.broadcast_to(sector_ref[:, piece].astype(jnp.int16), owner.shape), ones, zeros)
        for piece in pieces
    ]
    copies[1].wait()
    both = jnp.zeros((4 * bars, factors), jnp.float32)
    for index, piece in enumerate(pieces):
        copies[2 + 2 * index].wait()
        copies[3 + 2 * index].wait()
        loadings = loadings_ref[:, piece]
        scaled = loadings / variances_ref[:, piece]
        stacked = jnp.concatenate([returns_ref[:, piece] * scaled, scaled * loadings], axis=0)
        upper = stacked.astype(jnp.bfloat16)
        lower = (stacked - upper.astype(jnp.float32)).astype(jnp.bfloat16)
        both += lax.dot_general(
            jnp.concatenate([upper, lower], axis=0),
            one_hot[index],
            (((1,), (1,)), ((), ())),
            preferred_element_type=jnp.float32,
        )
    total = both[: 2 * bars] + both[2 * bars :]
    half = bars // 2
    low_lanes = lax.broadcasted_iota(jnp.int32, (half, LANES), 1) < HALF
    copies[-2].wait()
    copies[-1].wait()
    upper_half = jnp.full((half, LANES), row % 2, jnp.int32) == 1
    early, late = noise_ref[:half, :], noise_ref[half:, :]
    noise_out[...] = jnp.where(
        low_lanes,
        jnp.where(upper_half, pltpu.roll(early, HALF, 1), early),
        jnp.where(upper_half, late, pltpu.roll(late, HALF, 1)),
    )
    decay = decay_ref[...]
    decay_out[...] = jnp.where(low_lanes[:1] == upper_half[:1], pltpu.roll(decay, HALF, 1), decay)
    slots = row_order(peers)
    for pair in range(factors // LANES):
        columns = slice(pair * LANES, (pair + 1) * LANES)
        for kind in range(2):
            first = total[kind * bars : kind * bars + half, columns]
            second = total[kind * bars + half : (kind + 1) * bars, columns]
            rows = slice(kind * half, (kind + 1) * half)
            out_ref[slots.index(2 * pair), rows, :] = jnp.where(low_lanes, first, pltpu.roll(second, HALF, 1))
            out_ref[slots.index(2 * pair + 1), rows, :] = jnp.where(low_lanes, pltpu.roll(first, HALF, 1), second)


def added(terms):
    while len(terms) > 1:
        terms = [sum(terms[i + 1 : i + 2], terms[i]) for i in range(0, len(terms), 2)]
    return terms[0]


def block_kernel(parts_ref, noise_ref, decay_ref, local_ref, summary_ref):
    peers, rows, _ = parts_ref.shape
    half = rows // 2
    depth = half // SUB
    lane, sub = iotas()
    decay = decay_ref[...]
    elements = []
    for step in range(depth):
        signal = added([parts_ref[peer, pl.ds(step, SUB, stride=depth), :] for peer in range(peers)])
        information = added(
            [parts_ref[peer, pl.ds(half + step, SUB, stride=depth), :] for peer in range(peers)]
        )
        noise = noise_ref[pl.ds(step, SUB, stride=depth), :]
        inverse = 1.0 / (1.0 + noise * information)
        decayed = decay * inverse
        scaled = noise * inverse
        elements.append((decayed, scaled * signal, scaled, decayed * signal, decay * decayed * information))
    forward = [elements[0]]
    for step in range(1, depth):
        forward.append(combine(forward[-1], elements[step]))
    backward = [None] * depth
    running = elements[-1]
    for step in range(depth - 2, -1, -1):
        backward[step] = running
        running = combine(elements[step], running)
    total = forward[-1]
    ahead, behind = total, total
    for shift in (1, 2, 4):
        ahead = combine(keep(sub >= shift, rolled(ahead, shift, 0)), ahead)
        behind = combine(behind, keep(sub < SUB - shift, rolled(behind, SUB - shift, 0)))
    other = tuple(
        jnp.broadcast_to(pltpu.roll(part[SUB - 1 :, :], HALF, 1), (SUB, LANES)) for part in ahead
    )
    before = combine(keep(lane >= HALF, other), keep(sub >= 1, rolled(ahead, 1, 0)))
    after = combine(keep(sub < SUB - 1, rolled(behind, SUB - 1, 0)), keep(lane < HALF, other))
    whole = combine(other, ahead)
    low = lane[:1, :] < HALF
    rows = [part[SUB - 1 :, :] for part in whole]
    turned = [pltpu.roll(row, HALF, 1) for row in rows]
    packed = jnp.concatenate(
        [
            jnp.where(low, turned[0], rows[1]),
            jnp.where(low, turned[2], rows[3]),
            jnp.where(low, turned[4], rows[4]),
            jnp.zeros((1, LANES), jnp.float32),
        ],
        axis=0,
    )
    for peer in range(summary_ref.shape[0]):
        summary_ref[peer] = packed
    slot = 0
    for element in (before, after, *forward, *backward[:-1]):
        for part in element:
            local_ref[slot] = part
            slot += 1


def swapped(element, low):
    mask = lax.broadcasted_iota(jnp.int32, (1, LANES), 1) < HALF
    turn = rolled(element, HALF, 1)
    return tuple(
        jnp.where(mask, own, other) if low else jnp.where(mask, other, own) for own, other in zip(element, turn)
    )


def product(element):
    for shift in (1, 2, 4):
        element = combine(element, rolled(element, SUB - shift, 0))
    return tuple(part[:1, :] for part in element)


def finish_kernel(local_ref, received_ref, mean_ref, log_ref, sorted_ref):
    depth = (local_ref.shape[0] // 5 - 1) // 2
    place = lax.axis_index("tm")
    lane, sub = iotas()
    low = lane < HALF
    strip = received_ref.shape[0] // SUB
    for slot, block in enumerate(block_order(received_ref.shape[0])):
        sorted_ref[4 * block : 4 * block + 4, :] = received_ref[slot]
    pieces = []
    for step in range(strip):
        raw = [sorted_ref[pl.ds(4 * step + kind, SUB, stride=4 * strip), :] for kind in range(3)]
        turn = [pltpu.roll(part, HALF, 1) for part in raw[:2]]
        element = (
            jnp.where(low, raw[0], turn[0]),
            jnp.where(low, turn[0], raw[0]),
            jnp.where(low, raw[1], turn[1]),
            jnp.where(low, turn[1], raw[1]),
            raw[2],
        )
        block = sub * strip + step
        pieces.append(keep(jnp.where(low, block - place, place - block) < 0, element))
    while len(pieces) > 1:
        pieces = [combine(pieces[i], pieces[i + 1]) for i in range(0, len(pieces), 2)]
    total = product(pieces[0])
    before, after = swapped(total, True), swapped(total, False)
    mean_in, cov_in = before[1], before[2]
    info_in, prec_in = after[3], after[4]

    def element_at(index):
        return tuple(local_ref[5 * index + part] for part in range(5))

    def push(mean, cov, element):
        gain, shift_mean, shift_cov, info, prec = element
        scaled = gain / (1.0 + cov * prec)
        return scaled * (mean + cov * info) + shift_mean, scaled * gain * cov + shift_cov

    def pull(info, prec, element):
        gain, shift_mean, shift_cov, own_info, own_prec = element
        scaled = gain / (1.0 + shift_cov * prec)
        return scaled * (info - prec * shift_mean) + own_info, scaled * gain * prec + own_prec

    mean_in, cov_in = push(mean_in, cov_in, element_at(0))
    info_in, prec_in = pull(info_in, prec_in, element_at(1))
    for step in range(depth):
        mean, cov = push(mean_in, cov_in, element_at(2 + step))
        if step < depth - 1:
            info, prec = pull(info_in, prec_in, element_at(2 + depth + step))
        else:
            info, prec = info_in, prec_in
        inverse = 1.0 / (1.0 + cov * prec)
        smoothed = (mean + cov * info) * inverse
        logged = jnp.log(cov * inverse)
        for ref, value in ((mean_ref, smoothed), (log_ref, logged)):
            ref[pl.ds(step, SUB, stride=depth), :] = value[:, :HALF]
            ref[pl.ds(SUB * depth + step, SUB, stride=depth), :] = pltpu.roll(value, HALF, 1)[:, :HALF]


VMEM = pl.BlockSpec(memory_space=pltpu.VMEM)


SMALL = pltpu.CompilerParams(vmem_limit_bytes=4 * 1024 * 1024)


def exchanged(x, axis, order):
    return lax.all_to_all(x, axis, 0, 0, axis_index_groups=[order])


def body(returns, variances, loadings, sector, persistence, factor_noise):
    bars, series = returns.shape
    peers = lax.axis_size("rows")
    blocks = lax.axis_size("tm")
    half = bars // 2
    depth = half // SUB
    count = 2 * depth + 1
    inputs = [
        pltpu.with_memory_space_constraint(array, pltpu.HBM)
        for array in (
            returns, variances, loadings[None, :], sector[None, :], factor_noise, persistence[None, :]
        )
    ]
    sends, noise, decay = pl.pallas_call(
        project_kernel,
        out_shape=(
            pltpu.VMEM((peers, bars, LANES), jnp.float32),
            pltpu.VMEM((half, LANES), jnp.float32),
            pltpu.VMEM((1, LANES), jnp.float32),
        ),
        in_specs=[pl.BlockSpec(memory_space=pltpu.HBM)] * 6,
        out_specs=(VMEM, VMEM, VMEM),
        scratch_shapes=[
            pltpu.VMEM((bars, series), jnp.float32),
            pltpu.VMEM((bars, series), jnp.float32),
            pltpu.VMEM((1, series), jnp.float32),
            pltpu.VMEM((1, series), jnp.int32),
            pltpu.VMEM((bars, LANES), jnp.float32),
            pltpu.VMEM((1, LANES), jnp.float32),
            pltpu.SemaphoreType.DMA((4 + 2 * (series // PIECE),)),
        ],
        compiler_params=pltpu.CompilerParams(vmem_limit_bytes=24 * 1024 * 1024),
    )(*inputs)
    parts = exchanged(sends, "rows", row_order(peers))
    local, summary = pl.pallas_call(
        block_kernel,
        out_shape=(
            jax.ShapeDtypeStruct((5 * count, SUB, LANES), jnp.float32),
            jax.ShapeDtypeStruct((blocks, 4, LANES), jnp.float32),
        ),
        in_specs=[VMEM] * 3,
        out_specs=(VMEM, VMEM),
        compiler_params=SMALL,
    )(parts, noise, decay)
    received = exchanged(summary, "tm", block_order(blocks))
    return pl.pallas_call(
        finish_kernel,
        out_shape=(
            jax.ShapeDtypeStruct((bars, HALF), jnp.float32),
            jax.ShapeDtypeStruct((bars, HALF), jnp.float32),
        ),
        in_specs=[VMEM] * 2,
        out_specs=(VMEM, VMEM),
        scratch_shapes=[pltpu.VMEM((blocks * 4, LANES), jnp.float32)],
        compiler_params=SMALL,
    )(local, received)


def solution(mesh):
    in_specs = (P("tm", "rows"), P("tm", "rows"), P("rows"), P("rows"), P(), P("tm", None))
    out_specs = (P("tm", "rows"), P("tm", "rows"))
    return jax.shard_map(body, mesh=mesh, in_specs=in_specs, out_specs=out_specs, check_vma=False)
```
